256 devices in a mesh: dp: 16 (over y, x_hi, core), tensor: 16 (over z, x_lo).
Axes of the slice: x: 4 (x_hi: 2, x_lo: 2; x = x_hi * 2 + x_lo), y: 4, z: 8, core: 2. Of those that a mesh axis runs over, the one named last changes fastest.
Arguments:
- hidden: bfloat16 [8192, 8192], P('dp'), may hold values from -6 to 6
- query: bfloat16 [8192, 8192], P('dp', 'tensor'), may hold values from -300 to 300
- keys: bfloat16 [8192, 1024], P('dp', 'tensor'), may hold values from -18 to 18
- values: bfloat16 [8192, 1024], P('dp', 'tensor'), may hold values from -6 to 6
- grad_out: bfloat16 [8192, 8192], P('dp', 'tensor'), may hold values from -6 to 6
- key_weight: bfloat16 [8192, 1024], P('dp', 'tensor'), may hold values from -0.25 to 0.25
- value_weight: bfloat16 [8192, 1024], P('dp', 'tensor'), may hold values from -0.25 to 0.25
- lengths: int32 [16, 8], P('dp'), may hold values from 1 to 256, 512 in all within a row
Outputs:
- grad_query: bfloat16 [8192, 8192], P('dp', 'tensor')
- grad_hidden: bfloat16 [8192, 8192], P('dp', 'tensor')
- grad_key_weight: float32 [8192, 1024], P('dp', 'tensor')
- grad_value_weight: float32 [8192, 1024], P('dp', 'tensor')
The draws below stay inside these ranges and needn't reach their ends.
Inputs may be any that keep to these rules, and one draw needn't show every extreme that they name: `lengths`: each row sums to 512; its largest entry is exactly 256.
All inputs are finite; a program needn't handle non-finite values.
Results may differ from the reference program's by a relative error of at most 0.017.
Values may be sent and summed in bfloat16 or wider, within the bound.
A program may use at most 128 MiB of HBM per device.

```python
import math
import jax
import jax.numpy as jnp
import numpy as np
from jax import lax

D = 8192
HD = 128
GROUP = 8
KVH = 8
HQ = 64
TOK_DEV = 512
SEGS = 8
MOST = 256
TOKENS = 8192
N_DP = 16


def base_keys(key):
    return jnp.clip(jax.random.normal(key, (TOKENS, KVH * HD), jnp.float32), -6.0, 6.0)


def draw_keys(key, part):
    shared = base_keys(key)
    result = shared
    return result.astype(jnp.bfloat16)


def draw_query(key, part):
    key = jax.random.fold_in(key, 12)
    first_key = jax.random.fold_in(key, 0)
    drawn = jnp.clip(jax.random.normal(first_key, (TOKENS, HQ * HD), jnp.float32), -6.0, 6.0)
    result = drawn
    return result.astype(jnp.bfloat16)


def spiked(values, own_key, source, target, shards_of, factor):
    owner, partner = [(jnp.arange(values.shape[axis_at]) // (values.shape[axis_at] // shards_of)).reshape([-1 if axis == axis_at else 1 for axis in range(values.ndim)]) for axis_at in (source, target)]
    chosen = jax.random.permutation(own_key, shards_of)[partner]
    strong = (owner == chosen) | (owner == (partner + shards_of // 2) % shards_of)
    return jnp.where(strong, factor * values, values)


def shard_levels(own_key, shape, pieces, low, top_value):
    loudness = 1.0
    for dim, parts in pieces:
        heights = jax.random.uniform(jax.random.fold_in(jax.random.fold_in(own_key, 6), dim), (parts,), jnp.float32, low / len(pieces), top_value / len(pieces))
        loudness = loudness * jnp.repeat(jnp.exp(heights), shape[dim] // parts).reshape((-1,) + (1,) * (len(shape) - 1 - dim))
    return loudness


def profile(amount, total, most, skew):
    weights = [(1 << 20) // math.isqrt(grade ** skew) + 1 for grade in range(2, amount + 1)]
    rest, holding = total - most - (amount - 1), [1] * (amount - 1)
    while rest > 0:
        movable = [i for i in range(amount - 1) if holding[i] < most]
        mass, left = sum([weights[i] for i in movable]), rest
        for i in movable:
            addition = min(most - holding[i], max(1, left * weights[i] // mass), rest)
            holding[i] = holding[i] + addition
            rest = rest - addition
    return np.array([most] + holding)


def ragged(key, amount, total, bound, lean):
    if amount == 2:
        one = jax.random.randint(key, (), max(1, total - bound), min(bound, total - 1) + 1)
        return jnp.stack([one, total - one])
    tallies = jnp.asarray(profile(amount, total, bound, lean), jnp.int32)
    twos = (amount - 1) // 2
    source_of, sink = tallies[1:1 + 2 * twos:2], tallies[2:2 + 2 * twos:2]
    slack = jnp.minimum(source_of - 1, bound - sink)
    passed = jax.random.randint(jax.random.fold_in(key, 1), (twos,), 0, 1 << 20) % (slack + 1)
    tallies = tallies.at[1:1 + 2 * twos:2].set(source_of - passed).at[2:2 + 2 * twos:2].set(sink + passed)
    return tallies[jax.random.permutation(jax.random.fold_in(key, 2), amount)]


def centred(stream_key, shape, spread, reach, cuts=(), held_as=jnp.bfloat16):
    factor_of = shard_levels(stream_key, shape, cuts, -0.22, 0.18) if cuts else 1.0
    values = jax.random.normal(stream_key, shape, jnp.float32) * spread * factor_of
    return jnp.minimum(jnp.maximum(values, -reach), reach).astype(held_as)


def heavy_noise(stream_key, extent, width, reach, cuts, heavy, kind=jnp.bfloat16):
    entries = width * jax.random.normal(stream_key, extent, jnp.float32)
    if cuts:
        entries = entries * shard_levels(stream_key, extent, cuts, -0.22, 0.18)
    return jnp.clip(spiked(entries, jax.random.fold_in(stream_key, 3), *heavy), -reach, reach).astype(kind)


def setup_inputs(seed: int = 0) -> dict:
    seeds = jax.random.split(jax.random.key(seed), 9)
    hidden = heavy_noise(seeds[0], (TOKENS, D), 1.0, 6.0, ((0, 16),), (0, 1, 16, 2.0))
    query = draw_query(jax.random.fold_in(seeds[8], 71), 0)
    keys = draw_keys(jax.random.fold_in(seeds[8], 71), 0)
    values = centred(seeds[3], (TOKENS, KVH * HD), 1.0, 6.0, ((0, 16), (1, 16)))
    grad_out = centred(seeds[4], (TOKENS, HQ * HD), 1.0, 6.0, ((0, 16), (1, 16)))
    key_weight = heavy_noise(seeds[5], (D, KVH * HD), (KVH * HD) ** -0.5, 0.25, ((0, 16), (1, 16)), (1, 0, 16, 2.0))
    value_weight = heavy_noise(seeds[6], (D, KVH * HD), (KVH * HD) ** -0.5, 0.25, ((0, 16), (1, 16)), (1, 0, 16, 2.0))
    lengths = jax.vmap(lambda own: ragged(own, SEGS, TOK_DEV, MOST, 2))(jax.random.split(seeds[7], N_DP)).reshape((N_DP, SEGS)).astype(jnp.int32)
    return dict(hidden=hidden, query=query, keys=keys, values=values, grad_out=grad_out, key_weight=key_weight, value_weight=value_weight, lengths=lengths)


def block_backward(query, keys, values, grad_out, lengths):
    positions = jnp.arange(TOK_DEV, dtype=jnp.int32)
    bounds = jnp.cumsum(lengths).astype(jnp.int32)
    segment = jnp.sum((positions[:, None] >= bounds[None, :]).astype(jnp.int32), axis=1)
    allowed = (segment[:, None] == segment[None, :]) & (positions[None, :] <= positions[:, None])
    query_four = query.astype(jnp.float32).reshape(TOK_DEV, KVH, GROUP, HD)
    grad_four = grad_out.astype(jnp.float32).reshape(TOK_DEV, KVH, GROUP, HD)
    key_three = keys.astype(jnp.float32).reshape(TOK_DEV, KVH, HD)
    value_three = values.astype(jnp.float32).reshape(TOK_DEV, KVH, HD)
    score_scale = HD ** -0.5
    scores = jnp.einsum('ikgd,jkd->kgij', query_four, key_three) * score_scale
    scores = jnp.where(allowed[None, None], scores, -jnp.inf)
    top_score = jnp.max(scores, axis=-1, keepdims=True)
    expo = jnp.exp(scores - top_score)
    attn_probs = expo / jnp.sum(expo, axis=-1, keepdims=True)
    probs_low = lax.optimization_barrier(attn_probs.astype(jnp.bfloat16)).astype(jnp.float32)
    attended = jnp.einsum('kgij,jkd->ikgd', probs_low, value_three)
    row_delta = jnp.sum(grad_four * attended, axis=-1)
    dprobs = jnp.einsum('ikgd,jkd->kgij', grad_four, value_three)
    dscores = attn_probs * (dprobs - jnp.transpose(row_delta, (1, 2, 0))[..., None]) * score_scale
    dscores = lax.optimization_barrier(dscores.astype(jnp.bfloat16)).astype(jnp.float32)
    grad_query = jnp.einsum('kgij,jkd->ikgd', dscores, key_three).astype(jnp.bfloat16)
    key_grad = jnp.einsum('kgij,ikgd->jkd', dscores, query_four).astype(jnp.bfloat16)
    value_grad = jnp.einsum('kgij,ikgd->jkd', probs_low, grad_four).astype(jnp.bfloat16)
    return (grad_query.reshape(TOK_DEV, KVH * GROUP * HD), key_grad.reshape(TOK_DEV, KVH * HD),
            value_grad.reshape(TOK_DEV, KVH * HD))


def one_block(items):
    return block_backward(items[0], items[1], items[2], items[3], items[4])


def reference(hidden, query, keys, values, grad_out, key_weight, value_weight, lengths):
    blocks = (query.reshape(N_DP, TOK_DEV, HQ * HD), keys.reshape(N_DP, TOK_DEV, KVH * HD),
              values.reshape(N_DP, TOK_DEV, KVH * HD), grad_out.reshape(N_DP, TOK_DEV, HQ * HD), lengths)
    grad_query, key_grad, value_grad = lax.map(one_block, blocks)
    grad_query = grad_query.reshape(TOKENS, HQ * HD)
    key_grad = key_grad.reshape(TOKENS, KVH * HD)
    value_grad = value_grad.reshape(TOKENS, KVH * HD)
    grad_key_weight = jnp.dot(hidden.T, key_grad, preferred_element_type=jnp.float32)
    grad_value_weight = jnp.dot(hidden.T, value_grad, preferred_element_type=jnp.float32)
    grad_hidden = (jnp.dot(key_grad, key_weight.T, preferred_element_type=jnp.float32)
                   + jnp.dot(value_grad, value_weight.T, preferred_element_type=jnp.float32)).astype(jnp.bfloat16)
    return grad_query, grad_hidden, grad_key_weight, grad_value_weight
```

```python
import functools

import jax
import jax.numpy as jnp
from jax import lax
from jax.experimental import pallas as pl
from jax.experimental.pallas import tpu as pltpu
from jax.sharding import PartitionSpec as P

MESH = pl.DeviceIdType.MESH
F32 = jnp.float32
BF16 = jnp.bfloat16
TOK = 512
HEAD = 128
HALF = 64
HEADS = 4
ROWS = 128
STEPS = TOK // ROWS
FEAT = 512
NEG = -1e30

NT = (((1,), (1,)), ((), ()))
NN = (((1,), (0,)), ((), ()))
TN = (((0,), (0,)), ((), ()))


def dot(a, b, dims):
    return lax.dot_general(a, b, dims, preferred_element_type=F32)


NUMBER = {}
for name, count in (
    ("kv", 1),
    ("w_turn", 1),
    ("w_xh", 1),
    ("w_y", 6),
    ("w_core", 8),
    ("hid", 8),
    ("part", STEPS),
    ("kg_core", 2),
    ("ring_right", 8),
    ("ring_left", 8),
    ("c_y", 6),
    ("c_xh", 1),
    ("b_xl", STEPS),
):
    NUMBER[name] = sum(n for _, n in NUMBER.values()), count
N_REMOTE = sum(n for _, n in NUMBER.values())
LOCAL = {"k": 0, "v": 1, "kw": 2, "vw": 3, "q": 4, "go": 5, "hid": 6, "gq": 14, "gh": 15, "gk": 19, "gv": 20}
N_LOCAL = 21


def kernel(
    len_ref, hid_hbm, q_hbm, k_hbm, v_hbm, go_hbm, kw_hbm, vw_hbm,
    gq_hbm, gh_hbm, gk_hbm, gv_hbm,
    k_half, v_half, kw_half, vw_half, kv, key_buf, val_buf, q_buf, go_buf, gq_buf,
    w_own, w_all, hid_buf, dk_acc, dv_acc, part_send, part_got, keep_buf,
    kg_all, kg_other, kg_turned, c_send, c_got, c_own, cx_send, cx_got,
    b_send, b_got, b_own, gh_buf, gk_buf, gv_buf,
    send_sem, recv_sem, local_sem,
):
    dp, tensor = lax.axis_index("dp"), lax.axis_index("tensor")
    core, chip = lax.rem(dp, 2), dp // 2
    xh, y = lax.rem(chip, 2), chip // 2
    xl, z = lax.rem(tensor, 2), tensor // 2

    def at(y=y, xh=xh, core=core, z=z, xl=xl):
        return ((y * 2 + xh) * 2 + core, z * 2 + xl)

    def y_plus(k):
        return lax.rem(y + k, 4)

    def z_plus(k):
        return lax.rem(z + k + 8, 8)

    to_xl, to_core, to_xh = at(xl=1 - xl), at(core=1 - core), at(xh=1 - xh)
    to_right, to_left = at(z=z_plus(1)), at(z=z_plus(-1))
    to_y = [at(y=y_plus(k)) for k in (1, 2, 3)]
    to_turned = at(y=z // 2, xh=lax.rem(z, 2), z=chip)
    turned_away = chip != z

    def local(src, dst, number):
        copy = pltpu.make_async_copy(src, dst, local_sem.at[number])
        copy.start()
        return copy

    started = []

    def remote(src, dst, name, number, device):
        first, count = NUMBER[name]
        assert 0 <= number < count
        copy = pltpu.make_async_remote_copy(
            src_ref=src, dst_ref=dst, send_sem=send_sem.at[first + number],
            recv_sem=recv_sem.at[first + number], device_id=device, device_id_type=MESH,
        )
        return copy

    def send(*args):
        copy = remote(*args)
        copy.start()
        started.append(copy)

    def arrived(dst, name, number):
        first, _ = NUMBER[name]
        pltpu.make_async_remote_copy(
            src_ref=dst, dst_ref=dst, send_sem=send_sem.at[first + number],
            recv_sem=recv_sem.at[first + number], device_id=to_core, device_id_type=MESH,
        ).wait_recv()

    in_k = local(k_hbm, k_half, LOCAL["k"])
    in_v = local(v_hbm, v_half, LOCAL["v"])
    barrier = pltpu.get_barrier_semaphore()
    for device in [to_xl, to_core, to_xh, to_right, to_left] + to_y:
        pl.semaphore_signal(barrier, inc=1, device_id=device, device_id_type=MESH)

    @pl.when(turned_away)
    def _():
        pl.semaphore_signal(barrier, inc=1, device_id=to_turned, device_id_type=MESH)

    in_kw = local(kw_hbm, kw_half, LOCAL["kw"])
    in_vw = local(vw_hbm, vw_half, LOCAL["vw"])
    in_q = local(q_hbm, q_buf, LOCAL["q"])
    in_go = local(go_hbm, go_buf, LOCAL["go"])
    in_hid = []
    for block in range(8):
        columns = pl.ds(pl.multiple_of((2 * block + core) * FEAT, FEAT), FEAT)
        in_hid.append(local(hid_hbm.at[:, columns], hid_buf.at[block, 0], LOCAL["hid"] + block))
    in_k.wait()
    in_v.wait()
    kv[0] = jnp.concatenate([k_half[...], v_half[...]], axis=1)
    in_kw.wait()
    in_vw.wait()
    w_own[...] = jnp.concatenate([kw_half[...], vw_half[...]], axis=1)
    pl.semaphore_wait(barrier, 8 + jnp.where(turned_away, 1, 0))

    send(kv.at[0], kv.at[1], "kv", 0, to_xl)

    turn = remote(w_own, w_all.at[z, core], "w_turn", 0, to_turned)

    @pl.when(turned_away)
    def _():
        turn.start()

    for block in range(8):
        columns = pl.ds(pl.multiple_of((2 * block + 1 - core) * FEAT, FEAT), FEAT)
        send(hid_hbm.at[:, columns], hid_buf.at[block, 1], "hid", block, to_core)

    lane = lax.broadcasted_iota(jnp.int32, (1, HEADS * ROWS), 1) % ROWS
    bounds, total = [], 0
    for k in range(8):
        total = total + len_ref[0, k]
        bounds.append(total)

    def first_key(rows):
        start = jnp.zeros_like(rows)
        for bound in bounds:
            start = jnp.where(rows >= bound, bound, start)
        return start

    half_lane = lax.broadcasted_iota(jnp.int32, (1, HEAD), 1) < HALF
    lower = xl == 0
    dk_acc[...] = jnp.zeros_like(dk_acc)
    dv_acc[...] = jnp.zeros_like(dv_acc)

    arrived(kv.at[1], "kv", 0)
    own, other = kv[0].astype(F32), kv[1].astype(F32)
    first, second = jnp.where(lower, own, other), jnp.where(lower, other, own)
    key_buf[...] = jnp.where(half_lane, first, pltpu.roll(second, HALF, 1)).astype(BF16)
    val_buf[...] = jnp.where(half_lane, pltpu.roll(first, HALF, 1), second).astype(BF16)
    in_q.wait()
    in_go.wait()

    scale = HEAD ** -0.5
    to_exp2 = scale * 1.4426950408889634

    def heads_of(ref, step):
        return jnp.concatenate(
            [ref[pl.ds(step * ROWS, ROWS), pl.ds(h * HEAD, HEAD)] for h in range(HEADS)], axis=0
        )

    def attention(step):
        low, high = max(0, step - 2) * ROWS, (step + 1) * ROWS
        width = high - low
        seen = pl.ds(low, width)
        rows = lane + step * ROWS
        keys, vals = key_buf[seen, :], val_buf[seen, :]
        queries, grads = heads_of(q_buf, step), heads_of(go_buf, step)
        key_at = low + lax.broadcasted_iota(jnp.int32, (width, HEADS * ROWS), 0)
        allowed = (key_at >= first_key(rows)) & (key_at <= rows)
        scores = jnp.where(allowed, dot(keys, queries, NT), NEG)
        top = jnp.max(scores, axis=0, keepdims=True)
        expo = jnp.exp2((scores - top) * to_exp2)
        probs = expo * (1.0 / jnp.sum(expo, axis=0, keepdims=True))
        probs_low = probs.astype(BF16)
        dprobs = dot(vals, grads, NT)
        delta = jnp.sum(probs_low.astype(F32) * dprobs, axis=0, keepdims=True)
        dscores = (probs * (dprobs - delta) * scale).astype(BF16)
        grad_q = dot(dscores, keys, TN).astype(BF16)
        for h in range(HEADS):
            gq_buf[pl.ds(step * ROWS, ROWS), pl.ds(h * HEAD, HEAD)] = grad_q[h * ROWS:(h + 1) * ROWS]
        dk_acc[seen, :] += dot(dscores, queries, NN)
        dv_acc[seen, :] += dot(probs_low, grads, NN)
        done = pl.ds(step * ROWS, ROWS)
        dk, dv = dk_acc[done, :], dv_acc[done, :]
        lower_part = jnp.where(half_lane, dk, pltpu.roll(dv, HALF, 1))
        upper_part = jnp.where(half_lane, pltpu.roll(dk, HALF, 1), dv)
        keep_buf[done, :] = jnp.where(lower, lower_part, upper_part)
        part_send[done, :] = jnp.where(lower, upper_part, lower_part).astype(BF16)
        send(part_send.at[done], part_got.at[done], "part", step, to_xl)

    def finish(step):
        done = pl.ds(step * ROWS, ROWS)
        arrived(part_got.at[done], "part", step)
        kg_all[z, done, :] = (keep_buf[done, :] + part_got[done, :].astype(F32)).astype(BF16)

    def half_rows(half):
        return pl.ds(half * (TOK // 2), TOK // 2)

    def ring_hops(half):
        return (4, 3) if half == 1 else (3, 4)

    def ring_send(half, hop):
        rows = half_rows(half)
        right, left = ring_hops(half)
        if hop < right:
            block = kg_all.at[z_plus(-hop), rows]
            send(block, block, "ring_right", half * 4 + hop, to_right)
        if hop < left:
            block = kg_all.at[z_plus(hop), rows]
            send(block, block, "ring_left", half * 4 + hop, to_left)

    def ring_wait(half, hop):
        rows = half_rows(half)
        right, left = ring_hops(half)
        if hop < right:
            arrived(kg_all.at[z_plus(-hop - 1), rows], "ring_right", half * 4 + hop)
        if hop < left:
            arrived(kg_all.at[z_plus(hop + 1), rows], "ring_left", half * 4 + hop)

    def kg_start(half):
        rows = half_rows(half)
        ring_send(half, 0)
        send(kg_all.at[z, rows], kg_other.at[rows], "kg_core", half, to_core)

    def w_to_y(block, number):
        ref = w_all.at[block, core]
        for k in range(3):
            send(ref, ref, "w_y", number * 3 + k, to_y[k])

    def w_to_core(block, number):
        ref = w_all.at[block, core]
        send(ref, ref, "w_core", number, to_core)

    attention(3)

    @pl.when(turned_away)
    def _():
        arrived(w_all.at[chip, core], "w_turn", 0)

    @pl.when(jnp.logical_not(turned_away))
    def _():
        w_all[chip, core] = w_own[...]

    ref = w_all.at[chip, core]
    send(ref, ref, "w_xh", 0, to_xh)
    w_to_y(chip, 0)
    w_to_core(chip, 0)

    attention(2)
    attention(1)
    finish(3)
    finish(2)
    kg_start(1)
    chip_xh = y * 2 + 1 - xh
    arrived(w_all.at[chip_xh, core], "w_xh", 0)
    w_to_y(chip_xh, 1)
    w_to_core(chip_xh, 1)
    attention(0)
    out_gq = local(gq_buf, gq_hbm, LOCAL["gq"])
    finish(1)
    finish(0)
    kg_start(0)
    ring_wait(1, 0)
    ring_send(1, 1)

    for block in range(8):
        in_hid[block].wait()
        arrived(hid_buf.at[block, 1], "hid", block)
    arrived(kg_other.at[half_rows(1)], "kg_core", 1)
    arrived(kg_other.at[half_rows(0)], "kg_core", 0)
    kg_turned[:, pl.ds(0, TOK)] = kg_all[z].T
    kg_turned[:, pl.ds(TOK, TOK)] = kg_other[...].T

    def weight_grad(block):
        hid = hid_buf[block].reshape(2 * TOK, FEAT)
        return dot(kg_turned[...], hid, NN)

    def c_round(kind, x_high):
        for k in (2, 1, 3):
            number = kind * 3 + k - 1
            c_send[number] = weight_grad(y_plus(k) * 2 + x_high).astype(BF16)
            send(c_send.at[number], c_got.at[number], "c_y", number, to_y[k - 1])

    def c_sum(kind):
        total = c_own[kind]
        for k in range(3):
            arrived(c_got.at[kind * 3 + k], "c_y", kind * 3 + k)
            total = total + c_got[kind * 3 + k].astype(F32)
        return total

    c_round(0, 1 - xh)
    c_round(1, xh)
    ring_wait(0, 0)
    ring_send(0, 1)
    ring_wait(1, 1)
    ring_send(1, 2)
    c_own[0] = weight_grad(y * 2 + 1 - xh)
    c_own[1] = weight_grad(y * 2 + xh)
    ring_wait(0, 1)
    ring_send(0, 2)
    for k in range(3):
        for number, x_high in ((0, xh), (1, 1 - xh)):
            block = lax.rem(y - k - 1 + 4, 4) * 2 + x_high
            arrived(w_all.at[block, core], "w_y", number * 3 + k)
            w_to_core(block, 2 + number * 3 + k)
    ring_wait(1, 2)
    ring_send(1, 3)
    cx_send[...] = c_sum(0).astype(BF16)
    send(cx_send, cx_got, "c_xh", 0, to_xh)
    ring_wait(0, 2)
    ring_send(0, 3)
    arrived(w_all.at[chip, 1 - core], "w_core", 0)
    arrived(w_all.at[chip_xh, 1 - core], "w_core", 1)
    for k in range(3):
        for number, x_high in ((0, xh), (1, 1 - xh)):
            block = lax.rem(y - k - 1 + 4, 4) * 2 + x_high
            arrived(w_all.at[block, 1 - core], "w_core", 2 + number * 3 + k)

    def all_heads(rows):
        return jnp.concatenate([kg_all[head, rows, :] for head in range(8)], axis=1)

    def features(kind):
        return jnp.concatenate([w_all[head, kind] for head in range(8)], axis=1)

    def hidden_grad(half):
        for step in (2 * half + 1, 2 * half):
            rows = pl.ds(step * ROWS, ROWS)
            b_send[rows, :] = dot(all_heads(rows), features(1 - xl), NT).astype(BF16)
            send(b_send.at[rows], b_got.at[rows], "b_xl", step, to_xl)
        rows = half_rows(half)
        b_own[rows, :] = dot(all_heads(rows), features(xl), NT)

    ring_wait(1, 3)
    hidden_grad(1)
    ring_wait(0, 3)
    hidden_grad(0)

    mine = c_sum(1)
    arrived(cx_got, "c_xh", 0)
    mine = mine + cx_got[...].astype(F32)
    gk_buf[...] = mine[:HALF].T
    gv_buf[...] = mine[HALF:].T
    outs = [out_gq, local(gk_buf, gk_hbm, LOCAL["gk"]), local(gv_buf, gv_hbm, LOCAL["gv"])]
    for step in (3, 2, 1, 0):
        rows = pl.ds(step * ROWS, ROWS)
        arrived(b_got.at[rows], "b_xl", step)
        gh_buf[rows, :] = (b_own[rows, :] + b_got[rows, :].astype(F32)).astype(BF16)
        outs.append(local(gh_buf.at[rows], gh_hbm.at[rows], LOCAL["gh"] + step))
    for copy in outs:
        copy.wait()
    for copy in started:
        copy.wait_send()

    @pl.when(turned_away)
    def _():
        turn.wait_send()


def body(hidden, query, keys, values, grad_out, key_weight, value_weight, lengths):
    anywhere = pl.BlockSpec(memory_space=pl.ANY)

    def vmem(*shape, dtype=BF16):
        return pltpu.VMEM(shape, dtype)

    return pl.pallas_call(
        kernel,
        out_shape=(
            jax.ShapeDtypeStruct((TOK, HEADS * HEAD), BF16),
            jax.ShapeDtypeStruct((TOK, FEAT), BF16),
            jax.ShapeDtypeStruct((FEAT, HALF), F32),
            jax.ShapeDtypeStruct((FEAT, HALF), F32),
        ),
        in_specs=[pl.BlockSpec(memory_space=pltpu.SMEM)] + [anywhere] * 7,
        out_specs=(anywhere,) * 4,
        scratch_shapes=[
            vmem(TOK, HALF), vmem(TOK, HALF), vmem(FEAT, HALF), vmem(FEAT, HALF),
            vmem(2, TOK, HEAD), vmem(TOK, HEAD), vmem(TOK, HEAD),
            vmem(TOK, HEADS * HEAD), vmem(TOK, HEADS * HEAD), vmem(TOK, HEADS * HEAD),
            vmem(FEAT, HEAD), vmem(8, 2, FEAT, HEAD), vmem(8, 2, TOK, FEAT),
            vmem(TOK, HEAD, dtype=F32), vmem(TOK, HEAD, dtype=F32),
            vmem(TOK, HEAD), vmem(TOK, HEAD), vmem(TOK, HEAD, dtype=F32),
            vmem(8, TOK, HEAD), vmem(TOK, HEAD), vmem(HEAD, 2 * TOK),
            vmem(6, HEAD, FEAT), vmem(6, HEAD, FEAT), vmem(2, HEAD, FEAT, dtype=F32),
            vmem(HEAD, FEAT), vmem(HEAD, FEAT),
            vmem(TOK, FEAT), vmem(TOK, FEAT), vmem(TOK, FEAT, dtype=F32), vmem(TOK, FEAT),
            vmem(FEAT, HALF, dtype=F32), vmem(FEAT, HALF, dtype=F32),
            pltpu.SemaphoreType.DMA((N_REMOTE,)), pltpu.SemaphoreType.DMA((N_REMOTE,)),
            pltpu.SemaphoreType.DMA((N_LOCAL,)),
        ],
        compiler_params=pltpu.CompilerParams(
            collective_id=0, has_side_effects=True, vmem_limit_bytes=48 * 1024 * 1024
        ),
        name="attention_backward",
    )(lengths, hidden, query, keys, values, grad_out, key_weight, value_weight)


def solution(mesh):
    placed = (
        P("dp", None),
        P("dp", "tensor"),
        P("dp", "tensor"),
        P("dp", "tensor"),
        P("dp", "tensor"),
        P("dp", "tensor"),
        P("dp", "tensor"),
        P("dp", None),
    )
    return jax.shard_map(
        body,
        mesh=mesh,
        in_specs=placed,
        out_specs=(P("dp", "tensor"), P("dp", "tensor"), P("dp", "tensor"), P("dp", "tensor")),
        check_vma=False,
    )
```

```python
import functools

import jax
import jax.numpy as jnp
from jax import lax
from jax.experimental import pallas as pl
from jax.experimental.pallas import tpu as pltpu
from jax.sharding import PartitionSpec as P

MESH = pl.DeviceIdType.MESH
F32 = jnp.float32
BF16 = jnp.bfloat16
TOK = 512
HEAD = 128
HALF = 64
HEADS = 4
ROWS = 128
STEPS = TOK // ROWS
FEAT = 512
NEG = -1e30

NT = (((1,), (1,)), ((), ()))
NN = (((1,), (0,)), ((), ()))
TN = (((0,), (0,)), ((), ()))


def dot(a, b, dims):
    return lax.dot_general(a, b, dims, preferred_element_type=F32)


NUMBER = {}
for name, count in (
    ("kv", 2),
    ("w_turn", 3),
    ("w_y", 6),
    ("w_xh", 8),
    ("w_core", 16),
    ("hid", 8),
    ("part", STEPS),
    ("kg_core", STEPS),
    ("ring_right", 4 * STEPS),
    ("ring_left", 4 * STEPS),
    ("c_y", 6),
    ("c_xh", 1),
    ("b_xl", STEPS),
):
    NUMBER[name] = sum(n for _, n in NUMBER.values()), count
N_REMOTE = sum(n for _, n in NUMBER.values())
LOCAL = {"k": 0, "v": 1, "kw": 2, "vw": 3, "q": 4, "go": 5, "hid": 6, "gq": 14, "gh": 15, "gk": 19, "gv": 20, "mid": 21}
N_LOCAL = 22


def kernel(
    len_ref, hid_hbm, q_hbm, k_hbm, v_hbm, go_hbm, kw_hbm, vw_hbm,
    gq_hbm, gh_hbm, gk_hbm, gv_hbm,
    kv, key_buf, val_buf, q_buf, go_buf, gq_buf,
    w_all, w_mid, hid_buf, dk_acc, dv_acc, part_send, part_got, keep_buf,
    kg_all, kg_other, kg_turned, c_send, c_got, c_own, cx_send, cx_got,
    b_send, b_got, b_own, gh_buf, gk_buf, gv_buf,
    send_sem, recv_sem, local_sem,
):
    dp, tensor = lax.axis_index("dp"), lax.axis_index("tensor")
    core, chip = lax.rem(dp, 2), dp // 2
    xh, y = lax.rem(chip, 2), chip // 2
    xl, z = lax.rem(tensor, 2), tensor // 2

    def at(y=y, xh=xh, core=core, z=z, xl=xl):
        return ((y * 2 + xh) * 2 + core, z * 2 + xl)

    def y_plus(k):
        return lax.rem(y + k, 4)

    def z_plus(k):
        return lax.rem(z + k + 8, 8)

    to_xl, to_core, to_xh = at(xl=1 - xl), at(core=1 - core), at(xh=1 - xh)
    to_right, to_left = at(z=z_plus(1)), at(z=z_plus(-1))
    to_y = [at(y=y_plus(k)) for k in (1, 2, 3)]
    to_y_xh = [at(y=y_plus(k), xh=1 - xh) for k in (1, 2, 3)]
    turn_to = at(y=z // 2, xh=lax.rem(z, 2), z=chip)
    turn_away = chip != z
    ahead, behind = lax.rem(chip + z, 8), lax.rem(chip - z + 8, 8)
    mid_to = at(y=ahead // 2, xh=lax.rem(ahead, 2))
    mid_from = at(y=behind // 2, xh=lax.rem(behind, 2))
    mid_away = z != 0
    rise_to = at(z=behind)
    rise_away = behind != z

    def head_of(part, y, xh):
        return y * 2 + xh if part == 0 else lax.rem(y * 2 + xh - z + 8, 8)

    def local(src, dst, number):
        copy = pltpu.make_async_copy(src, dst, local_sem.at[number])
        copy.start()
        return copy

    started = []

    def remote(src, dst, name, number, device):
        first, count = NUMBER[name]
        assert 0 <= number < count
        copy = pltpu.make_async_remote_copy(
            src_ref=src, dst_ref=dst, send_sem=send_sem.at[first + number],
            recv_sem=recv_sem.at[first + number], device_id=device, device_id_type=MESH,
        )
        return copy

    def send(*args):
        copy = remote(*args)
        copy.start()
        started.append(copy)

    def arrived(dst, name, number):
        first, _ = NUMBER[name]
        pltpu.make_async_remote_copy(
            src_ref=dst, dst_ref=dst, send_sem=send_sem.at[first + number],
            recv_sem=recv_sem.at[first + number], device_id=to_core, device_id_type=MESH,
        ).wait_recv()

    low_half, high_half = pl.ds(0, HALF), pl.ds(HALF, HALF)
    parts = (low_half, high_half)
    barrier = pltpu.get_barrier_semaphore()
    for device in [to_xl, to_core, to_xh, to_right, to_left] + to_y + to_y_xh:
        pl.semaphore_signal(barrier, inc=1, device_id=device, device_id_type=MESH)

    for away, device in ((turn_away, turn_to), (mid_away, mid_from), (rise_away, rise_to)):

        @pl.when(away)
        def _():
            pl.semaphore_signal(barrier, inc=1, device_id=device, device_id_type=MESH)

    in_kv = [
        local(k_hbm, kv.at[0, low_half], LOCAL["k"]),
        local(v_hbm, kv.at[0, high_half], LOCAL["v"]),
    ]
    in_q = local(q_hbm, q_buf, LOCAL["q"])
    in_go = local(go_hbm, go_buf, LOCAL["go"])
    greeted = 11
    for away in (turn_away, mid_away, rise_away):
        greeted = greeted + jnp.where(away, 1, 0)
    pl.semaphore_wait(barrier, greeted)
    send(k_hbm, kv.at[1, low_half], "kv", 0, to_xl)
    send(v_hbm, kv.at[1, high_half], "kv", 1, to_xl)

    moves = []
    for number, (away, device, src, dst, name) in enumerate((
        (turn_away, turn_to, kw_hbm, w_all.at[core, z, low_half], "kw"),
        (mid_away, mid_to, vw_hbm, w_mid, "vw"),
        (rise_away, rise_to, w_mid, w_all.at[core, z, high_half], "mid"),
    )):
        stay = pltpu.make_async_copy(src, dst, local_sem.at[LOCAL[name]])
        moves.append((away, remote(src, dst, "w_turn", number, device), stay))

    def move_start(number):
        away, go, stay = moves[number]
        pl.when(away)(go.start)
        pl.when(jnp.logical_not(away))(stay.start)

    def move_wait(number, dst):
        away, _, stay = moves[number]
        pl.when(away)(lambda: arrived(dst, "w_turn", number))
        pl.when(jnp.logical_not(away))(stay.wait)

    move_start(0)
    move_start(1)
    in_hid = []
    for block in range(8):
        columns = pl.ds(pl.multiple_of((2 * block + core) * FEAT, FEAT), FEAT)
        in_hid.append(local(hid_hbm.at[:, columns], hid_buf.at[block, 0], LOCAL["hid"] + block))
    for block in range(8):
        columns = pl.ds(pl.multiple_of((2 * block + 1 - core) * FEAT, FEAT), FEAT)
        send(hid_hbm.at[:, columns], hid_buf.at[block, 1], "hid", block, to_core)

    lane = lax.broadcasted_iota(jnp.int32, (1, HEADS * ROWS), 1) % ROWS
    bounds, total = [], 0
    for k in range(8):
        total = total + len_ref[0, k]
        bounds.append(total)

    def first_key(rows):
        start = jnp.zeros_like(rows)
        for bound in bounds:
            start = jnp.where(rows >= bound, bound, start)
        return start

    half_lane = lax.broadcasted_iota(jnp.int32, (1, HEAD), 1) < HALF
    lower = xl == 0
    dk_acc[...] = jnp.zeros_like(dk_acc)
    dv_acc[...] = jnp.zeros_like(dv_acc)

    def whole_head(rows):
        own, other = kv[0, rows, :], kv[1, rows, :]
        first, second = jnp.where(lower, own, other), jnp.where(lower, other, own)
        return jnp.concatenate([first, second], axis=0).T

    scale = HEAD ** -0.5
    to_exp2 = scale * 1.4426950408889634

    def heads_of(ref, step):
        return jnp.concatenate(
            [ref[pl.ds(step * ROWS, ROWS), pl.ds(h * HEAD, HEAD)] for h in range(HEADS)], axis=0
        )

    def span(step):
        low = max(0, step - 2) * ROWS
        return low, (step + 1) * ROWS - low

    def softmax(step):
        low, width = span(step)
        rows = lane + step * ROWS
        key_at = low + lax.broadcasted_iota(jnp.int32, (width, HEADS * ROWS), 0)
        allowed = (key_at >= first_key(rows)) & (key_at <= rows)
        scores = dot(key_buf[pl.ds(low, width), :], heads_of(q_buf, step), NT)
        scores = jnp.where(allowed, scores, NEG)
        top = jnp.max(scores, axis=0, keepdims=True)
        expo = jnp.exp2((scores - top) * to_exp2)
        return expo * (1.0 / jnp.sum(expo, axis=0, keepdims=True))

    def gradients(step, probs):
        low, width = span(step)
        seen = pl.ds(low, width)
        queries, grads = heads_of(q_buf, step), heads_of(go_buf, step)
        dprobs = dot(val_buf[seen, :], grads, NT)
        probs_low = probs.astype(BF16)
        delta = jnp.sum(probs_low.astype(F32) * dprobs, axis=0, keepdims=True)
        dscores = (probs * (dprobs - delta) * scale).astype(BF16)
        grad_q = dot(dscores, key_buf[seen, :], TN).astype(BF16)
        for h in range(HEADS):
            gq_buf[pl.ds(step * ROWS, ROWS), pl.ds(h * HEAD, HEAD)] = grad_q[h * ROWS:(h + 1) * ROWS]
        dk_acc[seen, :] += dot(dscores, queries, NN)
        dv_acc[seen, :] += dot(probs_low, grads, NN)

    def part_out(step):
        done = pl.ds(step * ROWS, ROWS)
        dk, dv = dk_acc[done, :], dv_acc[done, :]
        lower_part = jnp.where(half_lane, dk, pltpu.roll(dv, HALF, 1))
        upper_part = jnp.where(half_lane, pltpu.roll(dk, HALF, 1), dv)
        keep_buf[done, :] = jnp.where(lower, lower_part, upper_part)
        part_send[done, :] = jnp.where(lower, upper_part, lower_part).astype(BF16)
        send(part_send.at[done], part_got.at[done], "part", step, to_xl)

    def finish(step):
        done = pl.ds(step * ROWS, ROWS)
        arrived(part_got.at[done], "part", step)
        kg_all[z, done, :] = (keep_buf[done, :] + part_got[done, :].astype(F32)).astype(BF16)

    def ring_hops(step):
        return (4, 3) if step >= 2 else (3, 4)

    def ring_send(step, hop):
        rows = pl.ds(step * ROWS, ROWS)
        right, left = ring_hops(step)
        if hop < right:
            block = kg_all.at[z_plus(-hop), rows]
            send(block, block, "ring_right", step * 4 + hop, to_right)
        if hop < left:
            block = kg_all.at[z_plus(hop), rows]
            send(block, block, "ring_left", step * 4 + hop, to_left)

    def ring_wait(step, hop):
        rows = pl.ds(step * ROWS, ROWS)
        right, left = ring_hops(step)
        if hop < right:
            arrived(kg_all.at[z_plus(-hop - 1), rows], "ring_right", step * 4 + hop)
        if hop < left:
            arrived(kg_all.at[z_plus(hop + 1), rows], "ring_left", step * 4 + hop)

    def kg_start(step):
        rows = pl.ds(step * ROWS, ROWS)
        ring_send(step, 0)
        send(kg_all.at[z, rows], kg_other.at[rows], "kg_core", step, to_core)

    def w_block(part, owner, y, xh):
        return w_all.at[owner, head_of(part, y, xh), parts[part]]

    def w_to_core(ref, part, number):
        send(ref, ref, "w_core", part * 8 + number, to_core)

    def w_enter(part):
        ref = w_block(part, core, y, xh)
        move_wait(2 * part, ref)
        for k in (1, 0, 2):
            send(ref, ref, "w_y", part * 3 + k, to_y[k])
        w_to_core(ref, part, 0)

    def w_across():
        ref = w_block(0, core, y, xh)
        send(ref, ref, "w_xh", 0, to_xh)
        for k in range(3):
            ref = w_block(0, core, y_plus(3 - k), xh)
            arrived(ref, "w_y", k)
            send(ref, ref, "w_xh", k + 1, to_xh)
            w_to_core(ref, 0, k + 1)
        w_enter(1)
        ref = w_block(1, core, y, xh)
        send(ref, ref, "w_xh", 4, to_xh)
        for k in (1, 0, 2):
            send(ref, ref, "w_xh", 5 + k, to_y_xh[k])

    def w_collect():
        for k in range(3):
            ref = w_block(1, core, y_plus(3 - k), xh)
            arrived(ref, "w_y", 3 + k)
            w_to_core(ref, 1, k + 1)
        for part in range(2):
            for k in range(4):
                ref = w_block(part, core, y_plus(4 - k), 1 - xh)
                arrived(ref, "w_xh", part * 4 + k)
                w_to_core(ref, part, 4 + k)

    def w_from_core(part):
        for k in range(4):
            arrived(w_block(part, 1 - core, y_plus(4 - k), xh), "w_core", part * 8 + k)
            arrived(w_block(part, 1 - core, y_plus(4 - k), 1 - xh), "w_core", part * 8 + 4 + k)

    in_kv[0].wait()
    arrived(kv.at[1, low_half], "kv", 0)
    key_buf[...] = whole_head(low_half)
    in_q.wait()
    probs = {step: softmax(step) for step in (3, 2)}
    move_wait(1, w_mid)
    move_start(2)
    in_kv[1].wait()
    arrived(kv.at[1, high_half], "kv", 1)
    val_buf[...] = whole_head(high_half)
    in_go.wait()
    for step in (3, 2):
        gradients(step, probs[step])
    for step in (3, 2):
        part_out(step)
    for step in (1, 0):
        gradients(step, softmax(step))
    for step in (1, 0):
        part_out(step)
    w_enter(0)
    out_gq = local(gq_buf, gq_hbm, LOCAL["gq"])
    for step in (3, 2, 1, 0):
        finish(step)
        kg_start(step)
    w_across()

    def ring_pass(hop, steps=(3, 2, 1, 0)):
        for step in steps:
            ring_wait(step, hop)
            ring_send(step, hop + 1)

    ring_pass(0)

    for block in range(8):
        in_hid[block].wait()
        arrived(hid_buf.at[block, 1], "hid", block)
    for step in (3, 2, 1, 0):
        rows = pl.ds(step * ROWS, ROWS)
        arrived(kg_other.at[rows], "kg_core", step)
    kg_turned[:, pl.ds(0, TOK)] = kg_all[z].T
    kg_turned[:, pl.ds(TOK, TOK)] = kg_other[...].T

    def weight_grad(block):
        hid = hid_buf[block].reshape(2 * TOK, FEAT)
        return dot(kg_turned[...], hid, NN)

    def c_round(kind, x_high):
        for k in (2, 1, 3):
            number = kind * 3 + k - 1
            c_send[number] = weight_grad(y_plus(k) * 2 + x_high).astype(BF16)
            send(c_send.at[number], c_got.at[number], "c_y", number, to_y[k - 1])

    def c_sum(kind):
        total = c_own[kind]
        for k in range(3):
            arrived(c_got.at[kind * 3 + k], "c_y", kind * 3 + k)
            total = total + c_got[kind * 3 + k].astype(F32)
        return total

    c_round(0, 1 - xh)
    ring_pass(1)
    c_round(1, xh)
    ring_pass(2)
    w_collect()
    c_own[0] = weight_grad(y * 2 + 1 - xh)
    c_own[1] = weight_grad(y * 2 + xh)
    w_from_core(0)
    w_from_core(1)

    def all_heads(rows):
        return jnp.concatenate([kg_all[head, rows, :] for head in range(8)], axis=1)

    def features(kind):
        return w_all[kind].reshape(8 * HEAD, FEAT)

    for step in (3, 2, 1, 0):
        rows = pl.ds(step * ROWS, ROWS)
        ring_wait(step, 3)
        b_send[rows, :] = dot(all_heads(rows), features(1 - xl), NN).astype(BF16)
        send(b_send.at[rows], b_got.at[rows], "b_xl", step, to_xl)
        if step == 2:
            cx_send[...] = c_sum(0).astype(BF16)
            send(cx_send, cx_got, "c_xh", 0, to_xh)
    b_own[...] = dot(all_heads(pl.ds(0, TOK)), features(xl), NN)

    mine = c_sum(1)
    arrived(cx_got, "c_xh", 0)
    mine = mine + cx_got[...].astype(F32)
    gk_buf[...] = mine[:HALF]
    gv_buf[...] = mine[HALF:]
    outs = [out_gq, local(gk_buf, gk_hbm, LOCAL["gk"]), local(gv_buf, gv_hbm, LOCAL["gv"])]
    for step in (3, 2, 1, 0):
        rows = pl.ds(step * ROWS, ROWS)
        arrived(b_got.at[rows], "b_xl", step)
        gh_buf[rows, :] = (b_own[rows, :] + b_got[rows, :].astype(F32)).astype(BF16)
        outs.append(local(gh_buf.at[rows], gh_hbm.at[rows], LOCAL["gh"] + step))
    for copy in outs:
        copy.wait()
    for copy in started:
        copy.wait_send()

    for away, go, _ in moves:
        pl.when(away)(go.wait_send)


def hand_over(*refs):
    for n in range(4):
        refs[4 + n][...] = refs[n][...]


def body(hidden, query, keys, values, grad_out, key_weight, value_weight, lengths):
    anywhere = pl.BlockSpec(memory_space=pl.ANY)

    def vmem(*shape, dtype=BF16):
        return pltpu.VMEM(shape, dtype)

    results = pl.pallas_call(
        kernel,
        out_shape=(
            jax.ShapeDtypeStruct((TOK, HEADS * HEAD), BF16),
            jax.ShapeDtypeStruct((TOK, FEAT), BF16),
            jax.ShapeDtypeStruct((HALF, FEAT), F32),
            jax.ShapeDtypeStruct((HALF, FEAT), F32),
        ),
        in_specs=[pl.BlockSpec(memory_space=pltpu.SMEM)] + [pl.BlockSpec(memory_space=pltpu.HBM)] * 7,
        out_specs=(anywhere,) * 4,
        scratch_shapes=[
            vmem(2, HEAD, TOK), vmem(TOK, HEAD), vmem(TOK, HEAD),
            vmem(TOK, HEADS * HEAD), vmem(TOK, HEADS * HEAD), vmem(TOK, HEADS * HEAD),
            vmem(2, 8, HEAD, FEAT), vmem(HALF, FEAT), vmem(8, 2, TOK, FEAT),
            vmem(TOK, HEAD, dtype=F32), vmem(TOK, HEAD, dtype=F32),
            vmem(TOK, HEAD), vmem(TOK, HEAD), vmem(TOK, HEAD, dtype=F32),
            vmem(8, TOK, HEAD), vmem(TOK, HEAD), vmem(HEAD, 2 * TOK),
            vmem(6, HEAD, FEAT), vmem(6, HEAD, FEAT), vmem(2, HEAD, FEAT, dtype=F32),
            vmem(HEAD, FEAT), vmem(HEAD, FEAT),
            vmem(TOK, FEAT), vmem(TOK, FEAT), vmem(TOK, FEAT, dtype=F32), vmem(TOK, FEAT),
            vmem(HALF, FEAT, dtype=F32), vmem(HALF, FEAT, dtype=F32),
            pltpu.SemaphoreType.DMA((N_REMOTE,)), pltpu.SemaphoreType.DMA((N_REMOTE,)),
            pltpu.SemaphoreType.DMA((N_LOCAL,)),
        ],
        compiler_params=pltpu.CompilerParams(
            collective_id=0, has_side_effects=True, vmem_limit_bytes=58 * 1024 * 1024
        ),
        name="attention_backward",
    )(lengths, hidden, query, keys.T, values.T, grad_out, key_weight.T, value_weight.T)
    grad_query, grad_hidden, key_turned, value_turned = pl.pallas_call(
        hand_over,
        out_shape=tuple(jax.ShapeDtypeStruct(r.shape, r.dtype) for r in results),
        compiler_params=pltpu.CompilerParams(vmem_limit_bytes=58 * 1024 * 1024),
        name="hand_over",
    )(*results)
    return grad_query, grad_hidden, key_turned.T, value_turned.T


def solution(mesh):
    placed = (
        P("dp", None),
        P("dp", "tensor"),
        P("dp", "tensor"),
        P("dp", "tensor"),
        P("dp", "tensor"),
        P("dp", "tensor"),
        P("dp", "tensor"),
        P("dp", None),
    )
    return jax.shard_map(
        body,
        mesh=mesh,
        in_specs=placed,
        out_specs=(P("dp", "tensor"), P("dp", "tensor"), P("dp", "tensor"), P("dp", "tensor")),
        check_vma=False,
    )
```

```python
import functools

import jax
import jax.numpy as jnp
from jax import lax
from jax.experimental import pallas as pl
from jax.experimental.pallas import tpu as pltpu
from jax.sharding import PartitionSpec as P

MESH = pl.DeviceIdType.MESH
F32 = jnp.float32
BF16 = jnp.bfloat16
TOK = 512
HEAD = 128
HALF = 64
HEADS = 4
ROWS = 128
STEPS = TOK // ROWS
FEAT = 512
NEG = -1e30

NT = (((1,), (1,)), ((), ()))
NN = (((1,), (0,)), ((), ()))
TN = (((0,), (0,)), ((), ()))


def dot(a, b, dims):
    return lax.dot_general(a, b, dims, preferred_element_type=F32)


NUMBER = {}
for name, count in (
    ("kv", 2),
    ("w_turn", 3),
    ("w_y", 6),
    ("w_xh", 1),
    ("w_core", 8),
    ("hid", 8),
    ("part", STEPS),
    ("kg_core", STEPS),
    ("ring_right", 4 * STEPS),
    ("ring_left", 4 * STEPS),
    ("c_y", 6),
    ("c_xh", 1),
    ("kg_xl", 8 * STEPS),
):
    NUMBER[name] = sum(n for _, n in NUMBER.values()), count
N_REMOTE = sum(n for _, n in NUMBER.values())
LOCAL = {"k": 0, "v": 1, "kw": 2, "vw": 3, "q": 4, "go": 5, "hid": 6, "gq": 14, "gh": 15, "gk": 19, "gv": 20, "len": 21, "mid": 22}
N_LOCAL = 23


def kernel(
    len_hbm, hid_hbm, q_hbm, k_hbm, v_hbm, go_hbm, kw_hbm, vw_hbm,
    gq_hbm, gh_hbm, gk_hbm, gv_hbm,
    kv, key_buf, val_buf, q_buf, go_buf, gq_buf,
    w_all, w_mid, hid_buf, dk_acc, dv_acc, part_send, part_got, keep_buf,
    kg_all, kg_other, kg_turned, c_send, c_got, c_own, cx_send, cx_got,
    b_own, gh_buf, gk_buf, gv_buf,
    len_ref, send_sem, recv_sem, local_sem,
):
    dp, tensor = lax.axis_index("dp"), lax.axis_index("tensor")
    core, chip = lax.rem(dp, 2), dp // 2
    xh, y = lax.rem(chip, 2), chip // 2
    xl, z = lax.rem(tensor, 2), tensor // 2

    def at(y=y, xh=xh, core=core, z=z, xl=xl):
        return ((y * 2 + xh) * 2 + core, z * 2 + xl)

    def y_plus(k):
        return lax.rem(y + k, 4)

    def z_plus(k):
        return lax.rem(z + k + 8, 8)

    to_xl, to_core, to_xh = at(xl=1 - xl), at(core=1 - core), at(xh=1 - xh)
    to_right, to_left = at(z=z_plus(1)), at(z=z_plus(-1))
    to_y = [at(y=y_plus(k)) for k in (1, 2, 3)]
    ahead, behind = lax.rem(chip + z, 8), lax.rem(chip - z + 8, 8)
    mid_to = at(y=ahead // 2, xh=lax.rem(ahead, 2))
    mid_from = at(y=behind // 2, xh=lax.rem(behind, 2))
    mid_away = z != 0
    rise_to = at(z=behind, core=xl, xl=core)
    rise_away = (behind != z) | (core != xl)

    def head_of(y, xh):
        return lax.rem(y * 2 + xh - z + 8, 8)

    def local(src, dst, number):
        copy = pltpu.make_async_copy(src, dst, local_sem.at[number])
        copy.start()
        return copy

    started = []

    def remote(src, dst, name, number, device):
        first, count = NUMBER[name]
        assert 0 <= number < count
        copy = pltpu.make_async_remote_copy(
            src_ref=src, dst_ref=dst, send_sem=send_sem.at[first + number],
            recv_sem=recv_sem.at[first + number], device_id=device, device_id_type=MESH,
        )
        return copy

    def send(*args):
        copy = remote(*args)
        copy.start()
        started.append(copy)

    def arrived(dst, name, number):
        first, _ = NUMBER[name]
        pltpu.make_async_remote_copy(
            src_ref=dst, dst_ref=dst, send_sem=send_sem.at[first + number],
            recv_sem=recv_sem.at[first + number], device_id=to_core, device_id_type=MESH,
        ).wait_recv()

    low_half, high_half = pl.ds(0, HALF), pl.ds(HALF, HALF)
    parts = (low_half, high_half)
    barrier = pltpu.get_barrier_semaphore()
    for device in [to_xl, to_core, to_xh, to_right, to_left] + to_y:
        pl.semaphore_signal(barrier, inc=1, device_id=device, device_id_type=MESH)

    for away, device in ((mid_away, mid_from), (rise_away, rise_to)):

        @pl.when(away)
        def _():
            pl.semaphore_signal(barrier, inc=1, device_id=device, device_id_type=MESH)

    in_kv = [
        local(k_hbm, kv.at[0, low_half], LOCAL["k"]),
        local(v_hbm, kv.at[0, high_half], LOCAL["v"]),
    ]
    in_len = local(len_hbm, len_ref, LOCAL["len"])
    in_q = local(q_hbm, q_buf, LOCAL["q"])
    in_go = local(go_hbm, go_buf, LOCAL["go"])
    pl.semaphore_wait(barrier, 8 + jnp.where(mid_away, 1, 0) + jnp.where(rise_away, 1, 0))
    send(k_hbm, kv.at[1, low_half], "kv", 0, to_xl)
    send(v_hbm, kv.at[1, high_half], "kv", 1, to_xl)

    moves = []
    for number, (away, device, src, dst, name) in enumerate((
        (mid_away, mid_to, kw_hbm, w_mid.at[low_half], "kw"),
        (mid_away, mid_to, vw_hbm, w_mid.at[high_half], "vw"),
        (rise_away, rise_to, w_mid, w_all.at[xl, z], "mid"),
    )):
        stay = pltpu.make_async_copy(src, dst, local_sem.at[LOCAL[name]])
        moves.append((away, remote(src, dst, "w_turn", number, device), stay))

    def move_start(number):
        away, go, stay = moves[number]
        pl.when(away)(go.start)
        pl.when(jnp.logical_not(away))(stay.start)

    def move_wait(number, dst):
        away, _, stay = moves[number]
        pl.when(away)(lambda: arrived(dst, "w_turn", number))
        pl.when(jnp.logical_not(away))(stay.wait)

    in_hid = []
    for block in range(8):
        columns = pl.ds(pl.multiple_of((2 * block + core) * FEAT, FEAT), FEAT)
        in_hid.append(local(hid_hbm.at[:, columns], hid_buf.at[block, 0], LOCAL["hid"] + block))
    for block in range(8):
        columns = pl.ds(pl.multiple_of((2 * block + 1 - core) * FEAT, FEAT), FEAT)
        send(hid_hbm.at[:, columns], hid_buf.at[block, 1], "hid", block, to_core)

    in_len.wait()
    lane = lax.broadcasted_iota(jnp.int32, (1, HEADS * ROWS), 1) % ROWS
    bounds, total = [], 0
    for k in range(8):
        total = total + len_ref[0, k]
        bounds.append(total)

    def first_key(rows):
        start = jnp.zeros_like(rows)
        for bound in bounds:
            start = jnp.where(rows >= bound, bound, start)
        return start

    half_lane = lax.broadcasted_iota(jnp.int32, (1, HEAD), 1) < HALF
    lower = xl == 0
    dk_acc[...] = jnp.zeros_like(dk_acc)
    dv_acc[...] = jnp.zeros_like(dv_acc)

    def whole_head(rows):
        own, other = kv[0, rows, :], kv[1, rows, :]
        first, second = jnp.where(lower, own, other), jnp.where(lower, other, own)
        return jnp.concatenate([first, second], axis=0).T

    scale = HEAD ** -0.5
    to_exp2 = scale * 1.4426950408889634

    def heads_of(ref, step):
        return jnp.concatenate(
            [ref[pl.ds(step * ROWS, ROWS), pl.ds(h * HEAD, HEAD)] for h in range(HEADS)], axis=0
        )

    def span(step):
        low = max(0, step - 2) * ROWS
        return low, (step + 1) * ROWS - low

    def softmax(step):
        low, width = span(step)
        rows = lane + step * ROWS
        key_at = low + lax.broadcasted_iota(jnp.int32, (width, HEADS * ROWS), 0)
        allowed = (key_at >= first_key(rows)) & (key_at <= rows)
        scores = dot(key_buf[pl.ds(low, width), :], heads_of(q_buf, step), NT)
        scores = jnp.where(allowed, scores, NEG)
        top = jnp.max(scores, axis=0, keepdims=True)
        expo = jnp.exp2((scores - top) * to_exp2)
        return expo * (1.0 / jnp.sum(expo, axis=0, keepdims=True))

    def gradients(step, probs):
        low, width = span(step)
        seen = pl.ds(low, width)
        queries, grads = heads_of(q_buf, step), heads_of(go_buf, step)
        dprobs = dot(val_buf[seen, :], grads, NT)
        probs_low = probs.astype(BF16)
        delta = jnp.sum(probs_low.astype(F32) * dprobs, axis=0, keepdims=True)
        dscores = (probs * (dprobs - delta) * scale).astype(BF16)
        grad_q = dot(dscores, key_buf[seen, :], TN).astype(BF16)
        for h in range(HEADS):
            gq_buf[pl.ds(step * ROWS, ROWS), pl.ds(h * HEAD, HEAD)] = grad_q[h * ROWS:(h + 1) * ROWS]
        dk_acc[seen, :] += dot(dscores, queries, NN)
        dv_acc[seen, :] += dot(probs_low, grads, NN)

    def part_out(step):
        done = pl.ds(step * ROWS, ROWS)
        dk, dv = dk_acc[done, :], dv_acc[done, :]
        lower_part = jnp.where(half_lane, dk, pltpu.roll(dv, HALF, 1))
        upper_part = jnp.where(half_lane, pltpu.roll(dk, HALF, 1), dv)
        keep_buf[done, :] = jnp.where(lower, lower_part, upper_part)
        part_send[done, :] = jnp.where(lower, upper_part, lower_part).astype(BF16)
        send(part_send.at[done], part_got.at[done], "part", step, to_xl)

    def finish(step):
        done = pl.ds(step * ROWS, ROWS)
        arrived(part_got.at[done], "part", step)
        kg_all[0, z, done, :] = (keep_buf[done, :] + part_got[done, :].astype(F32)).astype(BF16)

    def ring_hops(step):
        return (4, 3) if step >= 2 else (3, 4)

    def ring_send(step, hop):
        rows = pl.ds(step * ROWS, ROWS)
        right, left = ring_hops(step)
        if hop < right:
            block = kg_all.at[0, z_plus(-hop), rows]
            send(block, block, "ring_right", step * 4 + hop, to_right)
        if hop < left:
            block = kg_all.at[0, z_plus(hop), rows]
            send(block, block, "ring_left", step * 4 + hop, to_left)

    def ring_wait(step, hop):
        rows = pl.ds(step * ROWS, ROWS)
        right, left = ring_hops(step)
        if hop < right:
            arrived(kg_all.at[0, z_plus(-hop - 1), rows], "ring_right", step * 4 + hop)
        if hop < left:
            arrived(kg_all.at[0, z_plus(hop + 1), rows], "ring_left", step * 4 + hop)

    def across(step, number):
        head = z_plus((number + 1) // 2 * (1 if number % 2 else -1))
        rows = pl.ds(step * ROWS, ROWS)
        send(kg_all.at[0, head, rows], kg_all.at[1, head, rows], "kg_xl", step * 8 + number, to_xl)

    def kg_start(step):
        rows = pl.ds(step * ROWS, ROWS)
        ring_send(step, 0)
        across(step, 0)
        send(kg_all.at[0, z, rows], kg_other.at[rows], "kg_core", step, to_core)

    def w_block(owner, y, xh):
        return w_all.at[owner, head_of(y, xh)]

    def w_on(number, x_high):
        ref = w_block(core, y, x_high)
        for k in (1, 0, 2):
            send(ref, ref, "w_y", number * 3 + k, to_y[k])
        send(ref, ref, "w_core", number * 4, to_core)

    def w_enter():
        ref = w_block(core, y, xh)
        move_wait(2, ref)
        send(ref, ref, "w_xh", 0, to_xh)
        w_on(0, xh)

    def w_other_xh():
        arrived(w_block(core, y, 1 - xh), "w_xh", 0)
        w_on(1, 1 - xh)

    def w_from_y(number, x_high):
        for k in range(3):
            ref = w_block(core, y_plus(3 - k), x_high)
            arrived(ref, "w_y", number * 3 + k)
            send(ref, ref, "w_core", number * 4 + k + 1, to_core)

    def w_from_core():
        for number, x_high in ((0, xh), (1, 1 - xh)):
            for k in range(4):
                arrived(w_block(1 - core, y_plus(4 - k), x_high), "w_core", number * 4 + k)

    in_kv[0].wait()
    arrived(kv.at[1, low_half], "kv", 0)
    key_buf[...] = whole_head(low_half)
    in_q.wait()
    probs = {step: softmax(step) for step in (3, 2)}
    in_kv[1].wait()
    arrived(kv.at[1, high_half], "kv", 1)
    move_start(0)
    move_start(1)
    val_buf[...] = whole_head(high_half)
    in_go.wait()
    for step in (3, 2):
        gradients(step, probs[step])
    for step in (3, 2):
        part_out(step)
    for step in (1, 0):
        gradients(step, softmax(step))
    for step in (1, 0):
        part_out(step)
    out_gq = local(gq_buf, gq_hbm, LOCAL["gq"])
    for step in (3, 2, 1, 0):
        if step == 1:
            for number, rows in enumerate(parts):
                move_wait(number, w_mid.at[rows])
            move_start(2)
        finish(step)
        kg_start(step)

    def ring_pass(hop, steps=(3, 2, 1, 0)):
        for step in steps:
            ring_wait(step, hop)
            if hop < 3:
                ring_send(step, hop + 1)
            right, left = ring_hops(step)
            if hop < left:
                across(step, 2 * hop + 1)
            if hop < right:
                across(step, 2 * hop + 2 if hop < 3 else 7)


    for block in range(8):
        in_hid[block].wait()
        arrived(hid_buf.at[block, 1], "hid", block)
    for step in (3, 2, 1, 0):
        rows = pl.ds(step * ROWS, ROWS)
        arrived(kg_other.at[rows], "kg_core", step)
    kg_turned[:, pl.ds(0, TOK)] = kg_all[0, z].T
    kg_turned[:, pl.ds(TOK, TOK)] = kg_other[...].T

    def weight_grad(block):
        hid = hid_buf[block].reshape(2 * TOK, FEAT)
        return dot(kg_turned[...], hid, NN)

    def c_round(kind, x_high):
        for k in (2, 1, 3):
            number = kind * 3 + k - 1
            c_send[number] = weight_grad(y_plus(k) * 2 + x_high).astype(BF16)
            send(c_send.at[number], c_got.at[number], "c_y", number, to_y[k - 1])

    def c_sum(kind):
        total = c_own[kind]
        for k in range(3):
            arrived(c_got.at[kind * 3 + k], "c_y", kind * 3 + k)
            total = total + c_got[kind * 3 + k].astype(F32)
        return total

    c_round(0, 1 - xh)
    ring_pass(0)
    w_enter()
    c_round(1, xh)
    ring_pass(1)
    c_own[0] = weight_grad(y * 2 + 1 - xh)
    c_own[1] = weight_grad(y * 2 + xh)
    w_other_xh()
    ring_pass(2)
    cx_send[...] = c_sum(0).astype(BF16)
    send(cx_send, cx_got, "c_xh", 0, to_xh)
    ring_pass(3)
    w_from_y(0, xh)
    mine = c_sum(1)
    w_from_y(1, 1 - xh)
    w_from_core()

    def all_heads(line, rows):
        return jnp.concatenate([kg_all[line, head, rows, :] for head in range(8)], axis=1)

    def features(kind):
        return w_all[kind].reshape(8 * HEAD, FEAT)

    b_own[...] = dot(all_heads(0, pl.ds(0, TOK)), features(xl), NN)
    outs = [out_gq]
    for step in (3, 2, 1, 0):
        rows = pl.ds(step * ROWS, ROWS)
        for number in range(8):
            head = z_plus((number + 1) // 2 * (1 if number % 2 else -1))
            arrived(kg_all.at[1, head, rows], "kg_xl", step * 8 + number)
        gh_buf[rows, :] = (b_own[rows, :] + dot(all_heads(1, rows), features(1 - xl), NN)).astype(BF16)
        outs.append(local(gh_buf.at[rows], gh_hbm.at[rows], LOCAL["gh"] + step))
        if step == 1:
            arrived(cx_got, "c_xh", 0)
            mine = mine + cx_got[...].astype(F32)
            gk_buf[...] = mine[:HALF]
            gv_buf[...] = mine[HALF:]
            outs.append(local(gk_buf, gk_hbm, LOCAL["gk"]))
            outs.append(local(gv_buf, gv_hbm, LOCAL["gv"]))
    for copy in outs:
        copy.wait()
    for copy in started:
        copy.wait_send()

    for away, go, _ in moves:
        pl.when(away)(go.wait_send)


def hand_over(*refs):
    srcs, dsts, bufs, sems = refs[:4], refs[4:8], refs[8:12], refs[12]
    ins = [pltpu.make_async_copy(srcs[n], bufs[n], sems.at[n]) for n in range(4)]
    outs = [pltpu.make_async_copy(bufs[n], dsts[n], sems.at[4 + n]) for n in range(4)]
    for copy in ins:
        copy.start()
    for arriving, leaving in zip(ins, outs):
        arriving.wait()
        leaving.start()
    for copy in outs:
        copy.wait()


def body(hidden, query, keys, values, grad_out, key_weight, value_weight, lengths):
    anywhere = pl.BlockSpec(memory_space=pl.ANY)

    def vmem(*shape, dtype=BF16):
        return pltpu.VMEM(shape, dtype)

    results = pl.pallas_call(
        kernel,
        out_shape=(
            jax.ShapeDtypeStruct((TOK, HEADS * HEAD), BF16),
            jax.ShapeDtypeStruct((TOK, FEAT), BF16),
            jax.ShapeDtypeStruct((HALF, FEAT), F32),
            jax.ShapeDtypeStruct((HALF, FEAT), F32),
        ),
        in_specs=[pl.BlockSpec(memory_space=pltpu.HBM)] * 8,
        out_specs=(anywhere,) * 4,
        scratch_shapes=[
            vmem(2, HEAD, TOK), vmem(TOK, HEAD), vmem(TOK, HEAD),
            vmem(TOK, HEADS * HEAD), vmem(TOK, HEADS * HEAD), vmem(TOK, HEADS * HEAD),
            vmem(2, 8, HEAD, FEAT), vmem(HEAD, FEAT), vmem(8, 2, TOK, FEAT),
            vmem(TOK, HEAD, dtype=F32), vmem(TOK, HEAD, dtype=F32),
            vmem(TOK, HEAD), vmem(TOK, HEAD), vmem(TOK, HEAD, dtype=F32),
            vmem(2, 8, TOK, HEAD), vmem(TOK, HEAD), vmem(HEAD, 2 * TOK),
            vmem(6, HEAD, FEAT), vmem(6, HEAD, FEAT), vmem(2, HEAD, FEAT, dtype=F32),
            vmem(HEAD, FEAT), vmem(HEAD, FEAT),
            vmem(TOK, FEAT, dtype=F32), vmem(TOK, FEAT),
            vmem(HALF, FEAT, dtype=F32), vmem(HALF, FEAT, dtype=F32),
            pltpu.SMEM((1, 8), jnp.int32),
            pltpu.SemaphoreType.DMA((N_REMOTE,)), pltpu.SemaphoreType.DMA((N_REMOTE,)),
            pltpu.SemaphoreType.DMA((N_LOCAL,)),
        ],
        compiler_params=pltpu.CompilerParams(
            collective_id=0, has_side_effects=True, vmem_limit_bytes=58 * 1024 * 1024
        ),
        name="attention_backward",
    )(lengths, hidden, query, keys.T, values.T, grad_out, key_weight.T, value_weight.T)
    grad_query, grad_hidden, key_turned, value_turned = pl.pallas_call(
        hand_over,
        out_shape=tuple(jax.ShapeDtypeStruct(r.shape, r.dtype) for r in results),
        in_specs=[anywhere] * 4,
        out_specs=(anywhere,) * 4,
        scratch_shapes=[vmem(*r.shape, dtype=r.dtype) for r in results] + [pltpu.SemaphoreType.DMA((8,))],
        compiler_params=pltpu.CompilerParams(vmem_limit_bytes=58 * 1024 * 1024),
        name="hand_over",
    )(*results)
    return grad_query, grad_hidden, key_turned.T, value_turned.T


def solution(mesh):
    placed = (
        P("dp", None),
        P("dp", "tensor"),
        P("dp", "tensor"),
        P("dp", "tensor"),
        P("dp", "tensor"),
        P("dp", "tensor"),
        P("dp", "tensor"),
        P("dp", None),
    )
    return jax.shard_map(
        body,
        mesh=mesh,
        in_specs=placed,
        out_specs=(P("dp", "tensor"), P("dp", "tensor"), P("dp", "tensor"), P("dp", "tensor")),
        check_vma=False,
    )
```

```python
import functools

import jax
import jax.numpy as jnp
from jax import lax
from jax.experimental import pallas as pl
from jax.experimental.pallas import tpu as pltpu
from jax.sharding import PartitionSpec as P

MESH = pl.DeviceIdType.MESH
F32 = jnp.float32
BF16 = jnp.bfloat16
TOK = 512
HEAD = 128
HALF = 64
HEADS = 4
ROWS = 128
STEPS = TOK // ROWS
FEAT = 512
NEG = -1e30

NT = (((1,), (1,)), ((), ()))
NN = (((1,), (0,)), ((), ()))
TN = (((0,), (0,)), ((), ()))


def dot(a, b, dims):
    return lax.dot_general(a, b, dims, preferred_element_type=F32)


NUMBER = {}
for name, count in (
    ("kv", 2),
    ("w_turn", 3),
    ("w_y", 6),
    ("w_xh", 1),
    ("w_core", 8),
    ("hid", 8),
    ("part", STEPS),
    ("kg_core", STEPS),
    ("ring_right", 4 * STEPS),
    ("ring_left", 4 * STEPS),
    ("c_y", 6),
    ("c_xh", 1),
    ("kg_xl", 8 * STEPS),
):
    NUMBER[name] = sum(n for _, n in NUMBER.values()), count
N_REMOTE = sum(n for _, n in NUMBER.values())
LOCAL = {"k": 0, "v": 1, "kw": 2, "vw": 3, "q": 4, "go": 5, "hid": 6, "gq": 14, "gh": 15, "gk": 19, "gv": 20, "len": 21, "mid": 22}
N_LOCAL = 23


def kernel(
    len_hbm, hid_hbm, q_hbm, k_hbm, v_hbm, go_hbm, kw_hbm, vw_hbm,
    gq_hbm, gh_hbm, gk_hbm, gv_hbm,
    kv, key_buf, val_buf, q_buf, go_buf, gq_buf,
    w_all, w_mid, hid_buf, dk_acc, dv_acc, part_send, part_got, keep_buf,
    kg_all, kg_other, kg_turned, c_send, c_got, c_own, cx_send, cx_got,
    b_own, gh_buf, gk_buf, gv_buf,
    len_ref, send_sem, recv_sem, local_sem,
):
    dp, tensor = lax.axis_index("dp"), lax.axis_index("tensor")
    core, chip = lax.rem(dp, 2), dp // 2
    xh, y = lax.rem(chip, 2), chip // 2
    xl, z = lax.rem(tensor, 2), tensor // 2

    def at(y=y, xh=xh, core=core, z=z, xl=xl):
        return ((y * 2 + xh) * 2 + core, z * 2 + xl)

    def y_plus(k):
        return lax.rem(y + k, 4)

    def z_plus(k):
        return lax.rem(z + k + 8, 8)

    to_xl, to_core, to_xh = at(xl=1 - xl), at(core=1 - core), at(xh=1 - xh)
    to_right, to_left = at(z=z_plus(1)), at(z=z_plus(-1))
    to_y = [at(y=y_plus(k)) for k in (1, 2, 3)]
    ahead, behind = lax.rem(chip + z, 8), lax.rem(chip - z + 8, 8)
    mid_to = at(y=ahead // 2, xh=lax.rem(ahead, 2))
    mid_from = at(y=behind // 2, xh=lax.rem(behind, 2))
    mid_away = z != 0
    rise_to = at(z=behind, core=xl, xl=core)
    rise_away = (behind != z) | (core != xl)

    def head_of(y, xh):
        return lax.rem(y * 2 + xh - z + 8, 8)

    def local(src, dst, number):
        copy = pltpu.make_async_copy(src, dst, local_sem.at[number])
        copy.start()
        return copy

    started = []

    def remote(src, dst, name, number, device):
        first, count = NUMBER[name]
        assert 0 <= number < count
        copy = pltpu.make_async_remote_copy(
            src_ref=src, dst_ref=dst, send_sem=send_sem.at[first + number],
            recv_sem=recv_sem.at[first + number], device_id=device, device_id_type=MESH,
        )
        return copy

    def send(*args):
        copy = remote(*args)
        copy.start()
        started.append(copy)

    def arrived(dst, name, number):
        first, _ = NUMBER[name]
        pltpu.make_async_remote_copy(
            src_ref=dst, dst_ref=dst, send_sem=send_sem.at[first + number],
            recv_sem=recv_sem.at[first + number], device_id=to_core, device_id_type=MESH,
        ).wait_recv()

    low_half, high_half = pl.ds(0, HALF), pl.ds(HALF, HALF)
    parts = (low_half, high_half)
    barrier = pltpu.get_barrier_semaphore()
    for device in [to_xl, to_core, to_xh, to_right, to_left] + to_y:
        pl.semaphore_signal(barrier, inc=1, device_id=device, device_id_type=MESH)

    for away, device in ((mid_away, mid_from), (rise_away, rise_to)):

        @pl.when(away)
        def _():
            pl.semaphore_signal(barrier, inc=1, device_id=device, device_id_type=MESH)

    in_kv = [
        local(k_hbm, kv.at[0, low_half], LOCAL["k"]),
        local(v_hbm, kv.at[0, high_half], LOCAL["v"]),
    ]
    in_len = local(len_hbm, len_ref, LOCAL["len"])
    in_q = local(q_hbm, q_buf, LOCAL["q"])
    in_go = local(go_hbm, go_buf, LOCAL["go"])
    pl.semaphore_wait(barrier, 8 + jnp.where(mid_away, 1, 0) + jnp.where(rise_away, 1, 0))
    send(k_hbm, kv.at[1, low_half], "kv", 0, to_xl)
    send(v_hbm, kv.at[1, high_half], "kv", 1, to_xl)

    moves = []
    for number, (away, device, src, dst, name) in enumerate((
        (mid_away, mid_to, kw_hbm, w_mid.at[low_half], "kw"),
        (mid_away, mid_to, vw_hbm, w_mid.at[high_half], "vw"),
        (rise_away, rise_to, w_mid, w_all.at[xl, z], "mid"),
    )):
        stay = pltpu.make_async_copy(src, dst, local_sem.at[LOCAL[name]])
        moves.append((away, remote(src, dst, "w_turn", number, device), stay))

    def move_start(number):
        away, go, stay = moves[number]
        pl.when(away)(go.start)
        pl.when(jnp.logical_not(away))(stay.start)

    def move_wait(number, dst):
        away, _, stay = moves[number]
        pl.when(away)(lambda: arrived(dst, "w_turn", number))
        pl.when(jnp.logical_not(away))(stay.wait)

    in_hid = []
    for block in range(8):
        columns = pl.ds(pl.multiple_of((2 * block + core) * FEAT, FEAT), FEAT)
        in_hid.append(local(hid_hbm.at[:, columns], hid_buf.at[block, 0], LOCAL["hid"] + block))
    for block in range(8):
        columns = pl.ds(pl.multiple_of((2 * block + 1 - core) * FEAT, FEAT), FEAT)
        send(hid_hbm.at[:, columns], hid_buf.at[block, 1], "hid", block, to_core)

    in_len.wait()
    lane = lax.broadcasted_iota(jnp.int32, (1, HEADS * ROWS), 1) % ROWS
    bounds, total = [], 0
    for k in range(8):
        total = total + len_ref[0, k]
        bounds.append(total)

    def first_key(rows):
        start = jnp.zeros_like(rows)
        for bound in bounds:
            start = jnp.where(rows >= bound, bound, start)
        return start

    half_lane = lax.broadcasted_iota(jnp.int32, (1, HEAD), 1) < HALF
    lower = xl == 0
    dk_acc[...] = jnp.zeros_like(dk_acc)
    dv_acc[...] = jnp.zeros_like(dv_acc)

    def whole_head(rows):
        own, other = kv[0, rows, :], kv[1, rows, :]
        first, second = jnp.where(lower, own, other), jnp.where(lower, other, own)
        return jnp.concatenate([first, second], axis=0).T

    scale = HEAD ** -0.5
    to_exp2 = scale * 1.4426950408889634

    def heads_of(ref, step):
        return jnp.concatenate(
            [ref[pl.ds(step * ROWS, ROWS), pl.ds(h * HEAD, HEAD)] for h in range(HEADS)], axis=0
        )

    def span(step):
        low = max(0, step - 2) * ROWS
        return low, (step + 1) * ROWS - low

    def softmax(step):
        low, width = span(step)
        rows = lane + step * ROWS
        key_at = low + lax.broadcasted_iota(jnp.int32, (width, HEADS * ROWS), 0)
        allowed = (key_at >= first_key(rows)) & (key_at <= rows)
        scores = dot(key_buf[pl.ds(low, width), :], heads_of(q_buf, step), NT)
        scores = jnp.where(allowed, scores, NEG)
        top = jnp.max(scores, axis=0, keepdims=True)
        expo = jnp.exp2((scores - top) * to_exp2)
        return expo * (1.0 / jnp.sum(expo, axis=0, keepdims=True))

    def gradients(step, probs):
        low, width = span(step)
        seen = pl.ds(low, width)
        queries, grads = heads_of(q_buf, step), heads_of(go_buf, step)
        dprobs = dot(val_buf[seen, :], grads, NT)
        probs_low = probs.astype(BF16)
        delta = jnp.sum(probs_low.astype(F32) * dprobs, axis=0, keepdims=True)
        dscores = (probs * (dprobs - delta) * scale).astype(BF16)
        grad_q = dot(dscores, key_buf[seen, :], TN).astype(BF16)
        for h in range(HEADS):
            gq_buf[pl.ds(step * ROWS, ROWS), pl.ds(h * HEAD, HEAD)] = grad_q[h * ROWS:(h + 1) * ROWS]
        dk_acc[seen, :] += dot(dscores, queries, NN)
        dv_acc[seen, :] += dot(probs_low, grads, NN)

    def part_out(step):
        done = pl.ds(step * ROWS, ROWS)
        dk, dv = dk_acc[done, :], dv_acc[done, :]
        lower_part = jnp.where(half_lane, dk, pltpu.roll(dv, HALF, 1))
        upper_part = jnp.where(half_lane, pltpu.roll(dk, HALF, 1), dv)
        keep_buf[done, :] = jnp.where(lower, lower_part, upper_part)
        part_send[done, :] = jnp.where(lower, upper_part, lower_part).astype(BF16)
        send(part_send.at[done], part_got.at[done], "part", step, to_xl)

    def finish(step):
        done = pl.ds(step * ROWS, ROWS)
        arrived(part_got.at[done], "part", step)
        kg_all[0, z, done, :] = (keep_buf[done, :] + part_got[done, :].astype(F32)).astype(BF16)

    def ring_hops(step):
        return (4, 3) if step >= 2 else (3, 4)

    def ring_send(step, hop):
        rows = pl.ds(step * ROWS, ROWS)
        right, left = ring_hops(step)
        if hop < right:
            block = kg_all.at[0, z_plus(-hop), rows]
            send(block, block, "ring_right", step * 4 + hop, to_right)
        if hop < left:
            block = kg_all.at[0, z_plus(hop), rows]
            send(block, block, "ring_left", step * 4 + hop, to_left)

    def ring_wait(step, hop):
        rows = pl.ds(step * ROWS, ROWS)
        right, left = ring_hops(step)
        if hop < right:
            arrived(kg_all.at[0, z_plus(-hop - 1), rows], "ring_right", step * 4 + hop)
        if hop < left:
            arrived(kg_all.at[0, z_plus(hop + 1), rows], "ring_left", step * 4 + hop)

    def across(step, number):
        head = z_plus((number + 1) // 2 * (1 if number % 2 else -1))
        rows = pl.ds(step * ROWS, ROWS)
        send(kg_all.at[0, head, rows], kg_all.at[1, head, rows], "kg_xl", step * 8 + number, to_xl)

    def kg_start(step):
        rows = pl.ds(step * ROWS, ROWS)
        ring_send(step, 0)
        across(step, 0)
        send(kg_all.at[0, z, rows], kg_other.at[rows], "kg_core", step, to_core)

    def w_block(owner, y, xh):
        return w_all.at[owner, head_of(y, xh)]

    def w_on(number, x_high):
        ref = w_block(core, y, x_high)
        for k in (1, 0, 2):
            send(ref, ref, "w_y", number * 3 + k, to_y[k])
        send(ref, ref, "w_core", number * 4, to_core)

    def w_enter():
        ref = w_block(core, y, xh)
        move_wait(2, ref)
        send(ref, ref, "w_xh", 0, to_xh)
        w_on(0, xh)

    def w_other_xh():
        arrived(w_block(core, y, 1 - xh), "w_xh", 0)
        w_on(1, 1 - xh)

    def w_from_y(number, x_high):
        for k in range(3):
            ref = w_block(core, y_plus(3 - k), x_high)
            arrived(ref, "w_y", number * 3 + k)
            send(ref, ref, "w_core", number * 4 + k + 1, to_core)

    def w_from_core():
        for number, x_high in ((0, xh), (1, 1 - xh)):
            for k in range(4):
                arrived(w_block(1 - core, y_plus(4 - k), x_high), "w_core", number * 4 + k)

    in_kv[0].wait()
    arrived(kv.at[1, low_half], "kv", 0)
    key_buf[...] = whole_head(low_half)
    move_start(0)
    move_start(1)
    in_q.wait()
    probs = {step: softmax(step) for step in (3, 2)}
    in_kv[1].wait()
    arrived(kv.at[1, high_half], "kv", 1)
    val_buf[...] = whole_head(high_half)
    in_go.wait()
    for step in (3, 2):
        gradients(step, probs[step])
    for step in (3, 2):
        part_out(step)
    for step in (1, 0):
        gradients(step, softmax(step))
    for step in (1, 0):
        part_out(step)
    out_gq = local(gq_buf, gq_hbm, LOCAL["gq"])
    for number, rows in enumerate(parts):
        move_wait(number, w_mid.at[rows])
    move_start(2)
    for step in (3, 2, 1, 0):
        finish(step)
        kg_start(step)

    def ring_pass(hop, steps=(3, 2, 1, 0)):
        for step in steps:
            ring_wait(step, hop)
            if hop < 3:
                ring_send(step, hop + 1)
            right, left = ring_hops(step)
            if hop < left:
                across(step, 2 * hop + 1)
            if hop < right:
                across(step, 2 * hop + 2 if hop < 3 else 7)


    for block in range(8):
        in_hid[block].wait()
        arrived(hid_buf.at[block, 1], "hid", block)
    for step in (3, 2, 1, 0):
        rows = pl.ds(step * ROWS, ROWS)
        arrived(kg_other.at[rows], "kg_core", step)
    kg_turned[:, pl.ds(0, TOK)] = kg_all[0, z].T
    kg_turned[:, pl.ds(TOK, TOK)] = kg_other[...].T

    def weight_grad(block):
        hid = hid_buf[block].reshape(2 * TOK, FEAT)
        return dot(kg_turned[...], hid, NN)

    def c_round(kind, x_high):
        for k in (2, 1, 3):
            number = kind * 3 + k - 1
            c_send[number] = weight_grad(y_plus(k) * 2 + x_high).astype(BF16)
            send(c_send.at[number], c_got.at[number], "c_y", number, to_y[k - 1])

    def c_sum(kind):
        total = c_own[kind]
        for k in range(3):
            arrived(c_got.at[kind * 3 + k], "c_y", kind * 3 + k)
            total = total + c_got[kind * 3 + k].astype(F32)
        return total

    c_round(0, 1 - xh)
    ring_pass(0, (3, 2))
    w_enter()
    ring_pass(0, (1, 0))
    c_round(1, xh)
    ring_pass(1)
    c_own[0] = weight_grad(y * 2 + 1 - xh)
    c_own[1] = weight_grad(y * 2 + xh)
    w_other_xh()
    ring_pass(2)
    cx_send[...] = c_sum(0).astype(BF16)
    send(cx_send, cx_got, "c_xh", 0, to_xh)
    ring_pass(3)
    w_from_y(0, xh)
    mine = c_sum(1)
    w_from_y(1, 1 - xh)

    def all_heads(line, rows):
        return jnp.concatenate([kg_all[line, head, rows, :] for head in range(8)], axis=1)

    def features(kind):
        return w_all[kind].reshape(8 * HEAD, FEAT)

    for step in (3, 2, 1, 0):
        rows = pl.ds(step * ROWS, ROWS)
        for number in range(8):
            head = z_plus((number + 1) // 2 * (1 if number % 2 else -1))
            arrived(kg_all.at[1, head, rows], "kg_xl", step * 8 + number)
    first_line = jnp.where(core == xl, 0, 1)
    b_own[...] = dot(all_heads(first_line, pl.ds(0, TOK)), features(core), NN)
    w_from_core()
    outs = [out_gq]
    for step in (3, 2, 1, 0):
        rows = pl.ds(step * ROWS, ROWS)
        rest = dot(all_heads(1 - first_line, rows), features(1 - core), NN)
        gh_buf[rows, :] = (b_own[rows, :] + rest).astype(BF16)
        outs.append(local(gh_buf.at[rows], gh_hbm.at[rows], LOCAL["gh"] + step))
        if step == 1:
            arrived(cx_got, "c_xh", 0)
            mine = mine + cx_got[...].astype(F32)
            gk_buf[...] = mine[:HALF]
            gv_buf[...] = mine[HALF:]
            outs.append(local(gk_buf, gk_hbm, LOCAL["gk"]))
            outs.append(local(gv_buf, gv_hbm, LOCAL["gv"]))
    for copy in outs:
        copy.wait()
    for copy in started:
        copy.wait_send()

    for away, go, _ in moves:
        pl.when(away)(go.wait_send)


def hand_over(*refs):
    srcs, dsts, bufs, sems = refs[:4], refs[4:8], refs[8:12], refs[12]
    ins = [pltpu.make_async_copy(srcs[n], bufs[n], sems.at[n]) for n in range(4)]
    outs = [pltpu.make_async_copy(bufs[n], dsts[n], sems.at[4 + n]) for n in range(4)]
    for copy in ins:
        copy.start()
    for arriving, leaving in zip(ins, outs):
        arriving.wait()
        leaving.start()
    for copy in outs:
        copy.wait()


def body(hidden, query, keys, values, grad_out, key_weight, value_weight, lengths):
    anywhere = pl.BlockSpec(memory_space=pl.ANY)

    def vmem(*shape, dtype=BF16):
        return pltpu.VMEM(shape, dtype)

    results = pl.pallas_call(
        kernel,
        out_shape=(
            jax.ShapeDtypeStruct((TOK, HEADS * HEAD), BF16),
            jax.ShapeDtypeStruct((TOK, FEAT), BF16),
            jax.ShapeDtypeStruct((HALF, FEAT), F32),
            jax.ShapeDtypeStruct((HALF, FEAT), F32),
        ),
        in_specs=[pl.BlockSpec(memory_space=pltpu.HBM)] * 8,
        out_specs=(anywhere,) * 4,
        scratch_shapes=[
            vmem(2, HEAD, TOK), vmem(TOK, HEAD), vmem(TOK, HEAD),
            vmem(TOK, HEADS * HEAD), vmem(TOK, HEADS * HEAD), vmem(TOK, HEADS * HEAD),
            vmem(2, 8, HEAD, FEAT), vmem(HEAD, FEAT), vmem(8, 2, TOK, FEAT),
            vmem(TOK, HEAD, dtype=F32), vmem(TOK, HEAD, dtype=F32),
            vmem(TOK, HEAD), vmem(TOK, HEAD), vmem(TOK, HEAD, dtype=F32),
            vmem(2, 8, TOK, HEAD), vmem(TOK, HEAD), vmem(HEAD, 2 * TOK),
            vmem(6, HEAD, FEAT), vmem(6, HEAD, FEAT), vmem(2, HEAD, FEAT, dtype=F32),
            vmem(HEAD, FEAT), vmem(HEAD, FEAT),
            vmem(TOK, FEAT, dtype=F32), vmem(TOK, FEAT),
            vmem(HALF, FEAT, dtype=F32), vmem(HALF, FEAT, dtype=F32),
            pltpu.SMEM((1, 8), jnp.int32),
            pltpu.SemaphoreType.DMA((N_REMOTE,)), pltpu.SemaphoreType.DMA((N_REMOTE,)),
            pltpu.SemaphoreType.DMA((N_LOCAL,)),
        ],
        compiler_params=pltpu.CompilerParams(
            collective_id=0, has_side_effects=True, vmem_limit_bytes=58 * 1024 * 1024
        ),
        name="attention_backward",
    )(lengths, hidden, query, keys.T, values.T, grad_out, key_weight.T, value_weight.T)
    grad_query, grad_hidden, key_turned, value_turned = pl.pallas_call(
        hand_over,
        out_shape=tuple(jax.ShapeDtypeStruct(r.shape, r.dtype) for r in results),
        in_specs=[anywhere] * 4,
        out_specs=(anywhere,) * 4,
        scratch_shapes=[vmem(*r.shape, dtype=r.dtype) for r in results] + [pltpu.SemaphoreType.DMA((8,))],
        compiler_params=pltpu.CompilerParams(vmem_limit_bytes=58 * 1024 * 1024),
        name="hand_over",
    )(*results)
    return grad_query, grad_hidden, key_turned.T, value_turned.T


def solution(mesh):
    placed = (
        P("dp", None),
        P("dp", "tensor"),
        P("dp", "tensor"),
        P("dp", "tensor"),
        P("dp", "tensor"),
        P("dp", "tensor"),
        P("dp", "tensor"),
        P("dp", None),
    )
    return jax.shard_map(
        body,
        mesh=mesh,
        in_specs=placed,
        out_specs=(P("dp", "tensor"), P("dp", "tensor"), P("dp", "tensor"), P("dp", "tensor")),
        check_vma=False,
    )
```

```python
import functools

import jax
import jax.numpy as jnp
from jax import lax
from jax.experimental import pallas as pl
from jax.experimental.pallas import tpu as pltpu
from jax.sharding import PartitionSpec as P

MESH = pl.DeviceIdType.MESH
F32 = jnp.float32
BF16 = jnp.bfloat16
TOK = 512
HEAD = 128
HALF = 64
HEADS = 4
ROWS = 128
STEPS = TOK // ROWS
FEAT = 512
NEG = -1e30

NT = (((1,), (1,)), ((), ()))
NN = (((1,), (0,)), ((), ()))
TN = (((0,), (0,)), ((), ()))


def dot(a, b, dims):
    return lax.dot_general(a, b, dims, preferred_element_type=F32)


NUMBER = {}
for name, count in (
    ("kv", 2),
    ("w_turn", 3),
    ("w_y", 6),
    ("w_xh", 1),
    ("w_core", 8),
    ("hid", 8),
    ("part", STEPS),
    ("kg_core", STEPS),
    ("ring_right", 4 * STEPS),
    ("ring_left", 4 * STEPS),
    ("c_y", 6),
    ("c_xh", 1),
    ("kg_xl", 8 * STEPS),
):
    NUMBER[name] = sum(n for _, n in NUMBER.values()), count
N_REMOTE = sum(n for _, n in NUMBER.values())
LOCAL = {"k": 0, "v": 1, "kw": 2, "vw": 3, "q": 4, "go": 5, "hid": 6, "gq": 14, "gh": 15, "gk": 19, "gv": 20, "len": 21, "mid": 22}
N_LOCAL = 23


def kernel(
    len_hbm, hid_hbm, q_hbm, k_hbm, v_hbm, go_hbm, kw_hbm, vw_hbm,
    gq_hbm, gh_hbm, gk_hbm, gv_hbm,
    kv, key_buf, val_buf, q_buf, go_buf, gq_buf,
    w_all, w_mid, hid_buf, dk_acc, dv_acc, part_send, part_got, keep_buf,
    kg_all, kg_other, kg_turned, c_send, c_got, c_own, cx_send, cx_got,
    b_own, gh_buf, gk_buf, gv_buf,
    len_ref, send_sem, recv_sem, local_sem,
):
    dp, tensor = lax.axis_index("dp"), lax.axis_index("tensor")
    core, chip = lax.rem(dp, 2), dp // 2
    xh, y = lax.rem(chip, 2), chip // 2
    xl, z = lax.rem(tensor, 2), tensor // 2

    def at(y=y, xh=xh, core=core, z=z, xl=xl):
        return ((y * 2 + xh) * 2 + core, z * 2 + xl)

    def y_plus(k):
        return lax.rem(y + k, 4)

    def z_plus(k):
        return lax.rem(z + k + 8, 8)

    to_xl, to_core, to_xh = at(xl=1 - xl), at(core=1 - core), at(xh=1 - xh)
    to_right, to_left = at(z=z_plus(1)), at(z=z_plus(-1))
    to_y = [at(y=y_plus(k)) for k in (1, 2, 3)]
    ahead, behind = lax.rem(chip + z, 8), lax.rem(chip - z + 8, 8)
    mid_to = at(y=ahead // 2, xh=lax.rem(ahead, 2))
    mid_from = at(y=behind // 2, xh=lax.rem(behind, 2))
    mid_away = z != 0
    rise_to = at(z=behind, core=xl, xl=core)
    rise_away = (behind != z) | (core != xl)

    def head_of(y, xh):
        return lax.rem(y * 2 + xh - z + 8, 8)

    def local(src, dst, number):
        copy = pltpu.make_async_copy(src, dst, local_sem.at[number])
        copy.start()
        return copy

    started = []

    def remote(src, dst, name, number, device):
        first, count = NUMBER[name]
        assert 0 <= number < count
        copy = pltpu.make_async_remote_copy(
            src_ref=src, dst_ref=dst, send_sem=send_sem.at[first + number],
            recv_sem=recv_sem.at[first + number], device_id=device, device_id_type=MESH,
        )
        return copy

    def send(*args):
        copy = remote(*args)
        copy.start()
        started.append(copy)

    def arrived(dst, name, number):
        first, _ = NUMBER[name]
        pltpu.make_async_remote_copy(
            src_ref=dst, dst_ref=dst, send_sem=send_sem.at[first + number],
            recv_sem=recv_sem.at[first + number], device_id=to_core, device_id_type=MESH,
        ).wait_recv()

    low_half, high_half = pl.ds(0, HALF), pl.ds(HALF, HALF)
    parts = (low_half, high_half)
    barrier = pltpu.get_barrier_semaphore()
    for device in [to_xl, to_core, to_xh, to_right, to_left] + to_y:
        pl.semaphore_signal(barrier, inc=1, device_id=device, device_id_type=MESH)

    for away, device in ((mid_away, mid_from), (rise_away, rise_to)):

        @pl.when(away)
        def _():
            pl.semaphore_signal(barrier, inc=1, device_id=device, device_id_type=MESH)

    in_kv = [
        local(k_hbm, kv.at[0, low_half], LOCAL["k"]),
        local(v_hbm, kv.at[0, high_half], LOCAL["v"]),
    ]
    in_len = local(len_hbm, len_ref, LOCAL["len"])
    in_q = local(q_hbm, q_buf, LOCAL["q"])
    in_go = local(go_hbm, go_buf, LOCAL["go"])
    pl.semaphore_wait(barrier, 8 + jnp.where(mid_away, 1, 0) + jnp.where(rise_away, 1, 0))
    send(k_hbm, kv.at[1, low_half], "kv", 0, to_xl)
    send(v_hbm, kv.at[1, high_half], "kv", 1, to_xl)

    moves = []
    for number, (away, device, src, dst, name) in enumerate((
        (mid_away, mid_to, kw_hbm, w_mid.at[low_half], "kw"),
        (mid_away, mid_to, vw_hbm, w_mid.at[high_half], "vw"),
        (rise_away, rise_to, w_mid, w_all.at[xl, z], "mid"),
    )):
        stay = pltpu.make_async_copy(src, dst, local_sem.at[LOCAL[name]])
        moves.append((away, remote(src, dst, "w_turn", number, device), stay))

    def move_start(number):
        away, go, stay = moves[number]
        pl.when(away)(go.start)
        pl.when(jnp.logical_not(away))(stay.start)

    def move_wait(number, dst):
        away, _, stay = moves[number]
        pl.when(away)(lambda: arrived(dst, "w_turn", number))
        pl.when(jnp.logical_not(away))(stay.wait)

    in_hid = []
    for block in range(8):
        columns = pl.ds(pl.multiple_of((2 * block + core) * FEAT, FEAT), FEAT)
        in_hid.append(local(hid_hbm.at[:, columns], hid_buf.at[block, 0], LOCAL["hid"] + block))
    for block in range(8):
        columns = pl.ds(pl.multiple_of((2 * block + 1 - core) * FEAT, FEAT), FEAT)
        send(hid_hbm.at[:, columns], hid_buf.at[block, 1], "hid", block, to_core)

    in_len.wait()
    lane = lax.broadcasted_iota(jnp.int32, (1, HEADS * ROWS), 1) % ROWS
    bounds, total = [], 0
    for k in range(8):
        total = total + len_ref[0, k]
        bounds.append(total)

    def first_key(rows):
        start = jnp.zeros_like(rows)
        for bound in bounds:
            start = jnp.where(rows >= bound, bound, start)
        return start

    half_lane = lax.broadcasted_iota(jnp.int32, (1, HEAD), 1) < HALF
    lower = xl == 0
    dk_acc[...] = jnp.zeros_like(dk_acc)
    dv_acc[...] = jnp.zeros_like(dv_acc)

    def whole_head(rows):
        own, other = kv[0, rows, :], kv[1, rows, :]
        first, second = jnp.where(lower, own, other), jnp.where(lower, other, own)
        return jnp.concatenate([first, second], axis=0).T

    scale = HEAD ** -0.5
    to_exp2 = scale * 1.4426950408889634

    def heads_of(ref, step):
        return jnp.concatenate(
            [ref[pl.ds(step * ROWS, ROWS), pl.ds(h * HEAD, HEAD)] for h in range(HEADS)], axis=0
        )

    def span(step):
        low = max(0, step - 2) * ROWS
        return low, (step + 1) * ROWS - low

    def softmax(step):
        low, width = span(step)
        rows = lane + step * ROWS
        key_at = low + lax.broadcasted_iota(jnp.int32, (width, HEADS * ROWS), 0)
        allowed = (key_at >= first_key(rows)) & (key_at <= rows)
        scores = dot(key_buf[pl.ds(low, width), :], heads_of(q_buf, step), NT)
        scores = jnp.where(allowed, scores, NEG)
        top = jnp.max(scores, axis=0, keepdims=True)
        expo = jnp.exp2((scores - top) * to_exp2)
        return expo * (1.0 / jnp.sum(expo, axis=0, keepdims=True))

    def gradients(step, probs):
        low, width = span(step)
        seen = pl.ds(low, width)
        queries, grads = heads_of(q_buf, step), heads_of(go_buf, step)
        dprobs = dot(val_buf[seen, :], grads, NT)
        probs_low = probs.astype(BF16)
        delta = jnp.sum(probs_low.astype(F32) * dprobs, axis=0, keepdims=True)
        dscores = (probs * (dprobs - delta) * scale).astype(BF16)
        grad_q = dot(dscores, key_buf[seen, :], TN).astype(BF16)
        for h in range(HEADS):
            gq_buf[pl.ds(step * ROWS, ROWS), pl.ds(h * HEAD, HEAD)] = grad_q[h * ROWS:(h + 1) * ROWS]
        dk_acc[seen, :] += dot(dscores, queries, NN)
        dv_acc[seen, :] += dot(probs_low, grads, NN)

    def part_out(step):
        done = pl.ds(step * ROWS, ROWS)
        dk, dv = dk_acc[done, :], dv_acc[done, :]
        lower_part = jnp.where(half_lane, dk, pltpu.roll(dv, HALF, 1))
        upper_part = jnp.where(half_lane, pltpu.roll(dk, HALF, 1), dv)
        keep_buf[done, :] = jnp.where(lower, lower_part, upper_part)
        part_send[done, :] = jnp.where(lower, upper_part, lower_part).astype(BF16)
        send(part_send.at[done], part_got.at[done], "part", step, to_xl)

    def finish(step):
        done = pl.ds(step * ROWS, ROWS)
        arrived(part_got.at[done], "part", step)
        kg_all[0, z, done, :] = (keep_buf[done, :] + part_got[done, :].astype(F32)).astype(BF16)

    def ring_hops(step):
        return (4, 3) if step >= 2 else (3, 4)

    def ring_send(step, hop):
        rows = pl.ds(step * ROWS, ROWS)
        right, left = ring_hops(step)
        if hop < right:
            block = kg_all.at[0, z_plus(-hop), rows]
            send(block, block, "ring_right", step * 4 + hop, to_right)
        if hop < left:
            block = kg_all.at[0, z_plus(hop), rows]
            send(block, block, "ring_left", step * 4 + hop, to_left)

    def ring_wait(step, hop):
        rows = pl.ds(step * ROWS, ROWS)
        right, left = ring_hops(step)
        if hop < right:
            arrived(kg_all.at[0, z_plus(-hop - 1), rows], "ring_right", step * 4 + hop)
        if hop < left:
            arrived(kg_all.at[0, z_plus(hop + 1), rows], "ring_left", step * 4 + hop)

    def across(step, number):
        head = z_plus((number + 1) // 2 * (1 if number % 2 else -1))
        rows = pl.ds(step * ROWS, ROWS)
        send(kg_all.at[0, head, rows], kg_all.at[1, head, rows], "kg_xl", step * 8 + number, to_xl)

    def kg_start(step):
        rows = pl.ds(step * ROWS, ROWS)
        ring_send(step, 0)
        across(step, 0)
        send(kg_all.at[0, z, rows], kg_other.at[rows], "kg_core", step, to_core)

    def w_block(owner, y, xh):
        return w_all.at[owner, head_of(y, xh)]

    def w_on(number, x_high):
        ref = w_block(core, y, x_high)
        for k in (1, 0, 2):
            send(ref, ref, "w_y", number * 3 + k, to_y[k])
        send(ref, ref, "w_core", number * 4, to_core)

    def w_enter():
        ref = w_block(core, y, xh)
        move_wait(2, ref)
        send(ref, ref, "w_xh", 0, to_xh)
        w_on(0, xh)

    def w_other_xh():
        arrived(w_block(core, y, 1 - xh), "w_xh", 0)
        w_on(1, 1 - xh)

    def w_from_y(number, x_high):
        for k in range(3):
            ref = w_block(core, y_plus(3 - k), x_high)
            arrived(ref, "w_y", number * 3 + k)
            send(ref, ref, "w_core", number * 4 + k + 1, to_core)

    def w_from_core():
        for number, x_high in ((0, xh), (1, 1 - xh)):
            for k in range(4):
                arrived(w_block(1 - core, y_plus(4 - k), x_high), "w_core", number * 4 + k)

    in_kv[0].wait()
    arrived(kv.at[1, low_half], "kv", 0)
    key_buf[...] = whole_head(low_half)
    move_start(0)
    move_start(1)
    in_q.wait()
    probs = {step: softmax(step) for step in (3, 2)}
    in_kv[1].wait()
    arrived(kv.at[1, high_half], "kv", 1)
    val_buf[...] = whole_head(high_half)
    in_go.wait()
    for step in (3, 2):
        gradients(step, probs[step])
    for step in (3, 2):
        part_out(step)
    for step in (1, 0):
        gradients(step, softmax(step))
    for step in (1, 0):
        part_out(step)
    out_gq = local(gq_buf, gq_hbm, LOCAL["gq"])
    for number, rows in enumerate(parts):
        move_wait(number, w_mid.at[rows])
    move_start(2)
    for step in (3, 2, 1, 0):
        finish(step)
        kg_start(step)

    def ring_pass(hop, steps=(3, 2, 1, 0)):
        for step in steps:
            ring_wait(step, hop)
            if hop < 3:
                ring_send(step, hop + 1)
            right, left = ring_hops(step)
            if hop < left:
                across(step, 2 * hop + 1)
            if hop < right:
                across(step, 2 * hop + 2 if hop < 3 else 7)


    for block in range(8):
        in_hid[block].wait()
        arrived(hid_buf.at[block, 1], "hid", block)
    for step in (3, 2, 1, 0):
        rows = pl.ds(step * ROWS, ROWS)
        arrived(kg_other.at[rows], "kg_core", step)
    kg_turned[:, pl.ds(0, TOK)] = kg_all[0, z].T
    kg_turned[:, pl.ds(TOK, TOK)] = kg_other[...].T

    def weight_grad(block):
        hid = hid_buf[block].reshape(2 * TOK, FEAT)
        return dot(kg_turned[...], hid, NN)

    def c_round(kind, x_high):
        for k in (2, 1, 3):
            number = kind * 3 + k - 1
            c_send[number] = weight_grad(y_plus(k) * 2 + x_high).astype(BF16)
            send(c_send.at[number], c_got.at[number], "c_y", number, to_y[k - 1])

    def c_sum(kind):
        total = c_own[kind]
        for k in range(3):
            arrived(c_got.at[kind * 3 + k], "c_y", kind * 3 + k)
            total = total + c_got[kind * 3 + k].astype(F32)
        return total

    c_round(0, 1 - xh)
    ring_pass(0, (3, 2))
    w_enter()
    ring_pass(0, (1, 0))
    c_round(1, xh)
    ring_pass(1)
    c_own[0] = weight_grad(y * 2 + 1 - xh)
    c_own[1] = weight_grad(y * 2 + xh)
    w_other_xh()
    ring_pass(2)
    cx_send[...] = c_sum(0).astype(BF16)
    send(cx_send, cx_got, "c_xh", 0, to_xh)
    ring_pass(3)
    w_from_y(0, xh)
    mine = c_sum(1)
    w_from_y(1, 1 - xh)
    w_from_core()

    def all_heads(line, rows):
        return jnp.concatenate([kg_all[line, head, rows, :] for head in range(8)], axis=1)

    def features(kind):
        return w_all[kind].reshape(8 * HEAD, FEAT)

    b_own[...] = dot(all_heads(0, pl.ds(0, TOK)), features(xl), NN)
    outs = [out_gq]
    for step in (3, 2, 1, 0):
        rows = pl.ds(step * ROWS, ROWS)
        for number in range(8):
            head = z_plus((number + 1) // 2 * (1 if number % 2 else -1))
            arrived(kg_all.at[1, head, rows], "kg_xl", step * 8 + number)
        gh_buf[rows, :] = (b_own[rows, :] + dot(all_heads(1, rows), features(1 - xl), NN)).astype(BF16)
        outs.append(local(gh_buf.at[rows], gh_hbm.at[rows], LOCAL["gh"] + step))
        if step == 1:
            arrived(cx_got, "c_xh", 0)
            mine = mine + cx_got[...].astype(F32)
            gk_buf[...] = mine[:HALF]
            gv_buf[...] = mine[HALF:]
            outs.append(local(gk_buf, gk_hbm, LOCAL["gk"]))
            outs.append(local(gv_buf, gv_hbm, LOCAL["gv"]))
    for copy in outs:
        copy.wait()
    for copy in started:
        copy.wait_send()

    for away, go, _ in moves:
        pl.when(away)(go.wait_send)


def hand_over(*refs):
    srcs, dsts, bufs, sems = refs[:4], refs[4:8], refs[8:12], refs[12]
    ins = [pltpu.make_async_copy(srcs[n], bufs[n], sems.at[n]) for n in range(4)]
    outs = [pltpu.make_async_copy(bufs[n], dsts[n], sems.at[4 + n]) for n in range(4)]
    for copy in ins:
        copy.start()
    for arriving, leaving in zip(ins, outs):
        arriving.wait()
        leaving.start()
    for copy in outs:
        copy.wait()


def body(hidden, query, keys, values, grad_out, key_weight, value_weight, lengths):
    anywhere = pl.BlockSpec(memory_space=pl.ANY)

    def vmem(*shape, dtype=BF16):
        return pltpu.VMEM(shape, dtype)

    results = pl.pallas_call(
        kernel,
        out_shape=(
            jax.ShapeDtypeStruct((TOK, HEADS * HEAD), BF16),
            jax.ShapeDtypeStruct((TOK, FEAT), BF16),
            jax.ShapeDtypeStruct((HALF, FEAT), F32),
            jax.ShapeDtypeStruct((HALF, FEAT), F32),
        ),
        in_specs=[pl.BlockSpec(memory_space=pltpu.HBM)] * 8,
        out_specs=(anywhere,) * 4,
        scratch_shapes=[
            vmem(2, HEAD, TOK), vmem(TOK, HEAD), vmem(TOK, HEAD),
            vmem(TOK, HEADS * HEAD), vmem(TOK, HEADS * HEAD), vmem(TOK, HEADS * HEAD),
            vmem(2, 8, HEAD, FEAT), vmem(HEAD, FEAT), vmem(8, 2, TOK, FEAT),
            vmem(TOK, HEAD, dtype=F32), vmem(TOK, HEAD, dtype=F32),
            vmem(TOK, HEAD), vmem(TOK, HEAD), vmem(TOK, HEAD, dtype=F32),
            vmem(2, 8, TOK, HEAD), vmem(TOK, HEAD), vmem(HEAD, 2 * TOK),
            vmem(6, HEAD, FEAT), vmem(6, HEAD, FEAT), vmem(2, HEAD, FEAT, dtype=F32),
            vmem(HEAD, FEAT), vmem(HEAD, FEAT),
            vmem(TOK, FEAT, dtype=F32), vmem(TOK, FEAT),
            vmem(HALF, FEAT, dtype=F32), vmem(HALF, FEAT, dtype=F32),
            pltpu.SMEM((1, 8), jnp.int32),
            pltpu.SemaphoreType.DMA((N_REMOTE,)), pltpu.SemaphoreType.DMA((N_REMOTE,)),
            pltpu.SemaphoreType.DMA((N_LOCAL,)),
        ],
        compiler_params=pltpu.CompilerParams(
            collective_id=0, has_side_effects=True, vmem_limit_bytes=58 * 1024 * 1024
        ),
        name="attention_backward",
    )(lengths, hidden, query, keys.T, values.T, grad_out, key_weight.T, value_weight.T)
    grad_query, grad_hidden, key_turned, value_turned = pl.pallas_call(
        hand_over,
        out_shape=tuple(jax.ShapeDtypeStruct(r.shape, r.dtype) for r in results),
        in_specs=[anywhere] * 4,
        out_specs=(anywhere,) * 4,
        scratch_shapes=[vmem(*r.shape, dtype=r.dtype) for r in results] + [pltpu.SemaphoreType.DMA((8,))],
        compiler_params=pltpu.CompilerParams(vmem_limit_bytes=58 * 1024 * 1024),
        name="hand_over",
    )(*results)
    return grad_query, grad_hidden, key_turned.T, value_turned.T


def solution(mesh):
    placed = (
        P("dp", None),
        P("dp", "tensor"),
        P("dp", "tensor"),
        P("dp", "tensor"),
        P("dp", "tensor"),
        P("dp", "tensor"),
        P("dp", "tensor"),
        P("dp", None),
    )
    return jax.shard_map(
        body,
        mesh=mesh,
        in_specs=placed,
        out_specs=(P("dp", "tensor"), P("dp", "tensor"), P("dp", "tensor"), P("dp", "tensor")),
        check_vma=False,
    )
```
